128 devices in a mesh: dp: 8 (over y, x_lo), tensor: 8 (over z, core), pipe: 2 (over x_hi).
Axes of the slice: x: 4 (x_hi: 2, x_lo: 2; x = x_hi * 2 + x_lo), y: 4, z: 4, core: 2. Of those that a mesh axis runs over, the one named last changes fastest.
Arguments:
- attention_out: bfloat16 [2, 1024, 16384], P('pipe', 'dp', 'tensor'), may hold values from -6 to 6
- signs: int32 [2, 16384], P('pipe', 'tensor'), may hold values from -1 to 1, as said below
- out_weight: bfloat16 [2, 16384, 16384], P('pipe', 'tensor', 'dp'), may hold values from -0.046875 to 0.046875
- residual_in: bfloat16 [1024, 16384], P('tensor', 'dp'), may hold values from -6 to 6
Outputs:
- residual_out: bfloat16 [2, 1024, 16384], P('pipe', 'tensor', 'dp')
The draws below stay inside these ranges and needn't reach their ends.
Inputs may be any that keep to these rules, and one draw needn't show every extreme that they name: `signs`: each entry is 1 or -1.
All inputs are finite; a program needn't handle non-finite values.
Results may differ from the reference program's by a relative error of at most 0.018.
Values may be sent and summed in bfloat16 or wider, within the bound.
No kernel may reach another device: no remote copies, remote signals or barrier semaphores. Data moves between devices by JAX's collectives and lax.ppermute only.
A program may use at most 192 MiB of HBM per device.

```python
import math
import jax
import jax.numpy as jnp
from jax import lax

D = 16384
DW = 16384
TOKENS = 1024
SECTIONS = 2
N_TENSOR = 8


def draw_signs(key, part):
    key = jax.random.fold_in(key, 7)
    return (jax.random.randint(key, (SECTIONS, D), 0, 2) * 2 - 1).astype(jnp.int32)


def levels(key, shape, pieces, smallest, largest):
    level = 1.0
    for position, shards_of in pieces:
        draws = jax.random.uniform(jax.random.fold_in(jax.random.fold_in(key, 6), position), (shards_of,), jnp.float32, smallest / len(pieces), largest / len(pieces))
        level = level * jnp.repeat(jnp.exp(draws), shape[position] // shards_of).reshape((-1,) + (1,) * (len(shape) - 1 - position))
    return level


def gaussian(stream_key, dims, width, bound, shards=(), kind=jnp.bfloat16):
    entries = width * jax.random.normal(stream_key, dims, jnp.float32)
    if shards:
        entries = entries * levels(stream_key, dims, shards, -0.22, 0.18)
    return jnp.clip(entries, -bound, bound).astype(kind)


def setup_inputs(seed: int = 0) -> dict:
    keys = jax.random.split(jax.random.key(seed), 5)
    return {
        "attention_out": gaussian(keys[0], (SECTIONS, TOKENS, D), 1.0, 6.0, ((0, 2), (1, 8), (2, 8))),
        "signs": draw_signs(jax.random.fold_in(keys[4], 71), 0),
        "out_weight": gaussian(keys[2], (SECTIONS, D, DW), D ** -0.5, 0.046875, ((0, 2), (1, 8), (2, 8))),
        "residual_in": gaussian(keys[3], (TOKENS, DW), 1.0, 6.0, ((0, 8), (1, 8))),
    }


def hadamard_table(length, dtype):
    indices = jnp.arange(length, dtype=jnp.int32)
    common = indices[:, None] & indices[None, :]
    parity = jnp.zeros((length, length), jnp.int32)
    for bit_number in range(max(length.bit_length() - 1, 0)):
        parity = parity ^ common >> bit_number & 1
    return (1 - 2 * parity).astype(dtype)

def rotate(flipped, length):
    inner_size = min(length, 128)
    outer_size = length // inner_size
    blocks = flipped.astype(jnp.float32).reshape(flipped.shape[:-1] + (outer_size, inner_size))
    blocks = jnp.einsum('...ab,bc->...ac', blocks, hadamard_table(inner_size, jnp.float32), precision=lax.Precision.HIGHEST)
    blocks = jnp.einsum('...ab,ac->...cb', blocks, hadamard_table(outer_size, jnp.float32), precision=lax.Precision.HIGHEST)
    return blocks.reshape(flipped.shape)

def reference(attention_out, signs, out_weight, residual_in):
    norm_factor = jnp.float32(1.0 / math.sqrt(D))
    block_width = D // N_TENSOR
    current = residual_in.astype(jnp.float32)
    results = []
    for layer_index in range(SECTIONS):
        flipped = (attention_out[layer_index] * signs[layer_index].astype(jnp.bfloat16)[None, :]).astype(jnp.bfloat16)
        quantized = (rotate(flipped, D) * norm_factor).astype(jnp.bfloat16)
        projected = jnp.zeros((TOKENS, DW), jnp.float32)
        for member in range(N_TENSOR):
            partial_value = jnp.dot(quantized[:, member * block_width:(member + 1) * block_width], out_weight[layer_index, member * block_width:(member + 1) * block_width], preferred_element_type=jnp.float32).astype(jnp.bfloat16)
            projected = projected + partial_value.astype(jnp.float32)
        updated = (current + projected).astype(jnp.bfloat16)
        results.append(updated)
        current = lax.optimization_barrier(updated).astype(jnp.float32)
    return jnp.stack(results)
```

```python
import math

import jax
import jax.numpy as jnp
import numpy as np
from jax import lax
from jax.experimental import pallas as pl
from jax.experimental.pallas import tpu as pltpu
from jax.sharding import PartitionSpec as P

CHUNKS = 2
LANES = 128


def hadamard(length):
    table = np.array([[1]], np.int32)
    while table.shape[0] < length:
        table = np.block([[table, table], [table, -table]])
    return table


def move(value, axis, target):
    return lax.ppermute(value, axis, [(i, target(i)) for i in range(lax.axis_size(axis))])


def ring(steps, flip=0):
    return lambda i: (i // 2 + steps) % 4 * 2 + (i % 2 ^ flip)


def rotate_kernel(scale, x_ref, s_ref, h_ref, o_ref):
    rows, width = o_ref.shape
    pieces = width // LANES
    signs = s_ref[...].astype(jnp.float32)
    for r in range(0, rows, 32):
        part = []
        for a in range(pieces):
            cols = slice(a * LANES, (a + 1) * LANES)
            x = (x_ref[r : r + 32, cols].astype(jnp.float32) * signs[:, cols]).astype(jnp.bfloat16)
            part.append(jnp.dot(x, h_ref[...], preferred_element_type=jnp.float32))
        step = 1
        while step < pieces:
            nxt = list(part)
            for a in range(pieces):
                if not a & step:
                    nxt[a] = part[a] + part[a | step]
                    nxt[a | step] = part[a] - part[a | step]
            part = nxt
            step *= 2
        for a in range(pieces):
            o_ref[r : r + 32, a * LANES : (a + 1) * LANES] = (part[a] * scale).astype(jnp.bfloat16)


def rotate_local(x, signs, scale):
    return pl.pallas_call(
        lambda *refs: rotate_kernel(scale, *refs),
        out_shape=jax.ShapeDtypeStruct(x.shape, jnp.bfloat16),
        compiler_params=pltpu.CompilerParams(vmem_limit_bytes=16 << 20),
        cost_estimate=pl.CostEstimate(flops=2 * x.size * LANES, bytes_accessed=4 * x.size, transcendentals=0),
        name="rotate_local",
    )(x, signs.reshape(1, -1), jnp.asarray(hadamard(LANES), jnp.bfloat16))


def project_kernel(slot_ref, *refs):
    blocks, (w_ref, keep_ref, send_ref, lhs) = refs[:8], refs[8:]
    rows = blocks[0].shape[0]

    @pl.when(pl.program_id(0) == 0)
    def _():
        for i, ref in enumerate(blocks):
            start = pl.multiple_of(slot_ref[i] * rows, rows)
            lhs[pl.ds(start, rows), :] = ref[...]

    out = jnp.dot(lhs[...], w_ref[...], preferred_element_type=jnp.float32).astype(jnp.bfloat16)
    keep_ref[...] = out[: 4 * rows]
    send_ref[...] = out[4 * rows :]


def project(slots, blocks, weight, tile=512):
    rows, depth = blocks[0].shape
    width = weight.shape[1]
    half = jax.ShapeDtypeStruct((4 * rows, width), jnp.bfloat16)
    whole = pl.BlockSpec((rows, depth), lambda n, s: (0, 0))
    out = pl.BlockSpec((4 * rows, tile), lambda n, s: (0, n))
    return pl.pallas_call(
        project_kernel,
        out_shape=(half, half),
        grid_spec=pltpu.PrefetchScalarGridSpec(
            num_scalar_prefetch=1,
            grid=(width // tile,),
            in_specs=[whole] * 8 + [pl.BlockSpec((depth, tile), lambda n, s: (0, n))],
            out_specs=(out, out),
            scratch_shapes=[pltpu.VMEM((8 * rows, depth), jnp.bfloat16)],
        ),
        compiler_params=pltpu.CompilerParams(vmem_limit_bytes=32 << 20),
        cost_estimate=pl.CostEstimate(
            flops=2 * 8 * rows * depth * width, bytes_accessed=2 * (depth * width + 16 * rows * depth), transcendentals=0
        ),
        name="project",
    )(slots, *blocks, weight)


def f32(value):
    return value.astype(jnp.float32)


def after(value, earlier):
    return lax.optimization_barrier((value, earlier))[0]


def on_device(attention_out, signs, out_weight, residual_in):
    d, t = lax.axis_index("dp"), lax.axis_index("tensor")
    y, x, z, c = d // 2, d % 2, t // 2, t % 2
    first = lax.axis_index("pipe") == 0
    width = attention_out.shape[2]
    scale = 1.0 / math.sqrt(width * lax.axis_size("tensor"))
    weight = out_weight[0]

    local = rotate_local(attention_out[0], signs[0], scale)
    other = move(local, "tensor", lambda i: i ^ 1)
    paired = (f32(other) + (1 - 2 * c).astype(jnp.float32) * f32(local)).astype(jnp.bfloat16)

    def sign(k):
        u = z & ((z + k) % 4)
        return (1 - 2 * ((u ^ (u >> 1)) & 1)).astype(jnp.float32)

    rows = attention_out.shape[1] // CHUNKS
    slots = []
    for dy, dx in ORDER:
        by, bx = (y + dy) % 4, x ^ dx
        slots.append(((bx ^ c) * 4 + (by - z) % 4).astype(jnp.int32))
    slots = jnp.stack(slots)

    result = []
    for chunk in range(CHUNKS):
        at = slice(chunk * rows, (chunk + 1) * rows)
        mine = paired[at]
        terms = [mine] + [move(mine, "tensor", ring(-k)) for k in (1, 3, 2)]
        if chunk:
            terms = after(terms, own)
        total = f32(terms[0]) * sign(0)
        for k, term in zip((1, 3, 2), terms[1:]):
            total = total + f32(term) * sign(k)
        own = total.astype(jnp.bfloat16)

        got = {(0, 0): own}
        got[0, 1] = move(own, "dp", ring(0, 1))
        for dy in (1, 3, 2):
            got[dy, 0] = move(own, "dp", ring(-dy))
        for dy in (1, 3):
            got[dy, 1] = move(got[0, 1], "dp", ring(-dy))
        got[2, 1] = move(got[2, 0], "dp", ring(0, 1))

        keep, send = project(slots, [got[o] for o in ORDER], weight)
        came = move(send, "tensor", lambda i: i ^ 1)
        if chunk:
            keep, came = after((keep, came), leading)

        def part(k):
            return f32(keep[k * rows : (k + 1) * rows]) + f32(came[k * rows : (k + 1) * rows])

        summed = part(0)
        for k in (1, 3, 2):
            summed = summed + f32(move(part(k).astype(jnp.bfloat16), "tensor", ring(k)))
        leading = (f32(residual_in[at]) + summed).astype(jnp.bfloat16)
        passed = lax.ppermute(leading, "pipe", [(0, 1)])
        downstream = (f32(passed) + summed).astype(jnp.bfloat16)
        result.append(jnp.where(first, leading, downstream))
    return jnp.concatenate(result, axis=0)[None]


ORDER = [(0, 0), (0, 1), (1, 0), (3, 0), (2, 0), (1, 1), (3, 1), (2, 1)]


def solution(mesh):
    in_specs = (
        P("pipe", "dp", "tensor"),
        P("pipe", "tensor"),
        P("pipe", "tensor", "dp"),
        P("tensor", "dp"),
    )
    out_specs = P("pipe", "tensor", "dp")
    return jax.shard_map(
        on_device, mesh=mesh, in_specs=in_specs, out_specs=out_specs, check_vma=False
    )
```

```python
import math

import jax
import jax.numpy as jnp
from jax import lax
from jax.experimental import pallas as pl
from jax.experimental.pallas import tpu as pltpu
from jax.sharding import PartitionSpec as P

LANES = 128
BF16 = jnp.bfloat16
TILES = 4


def f32(value):
    return value.astype(jnp.float32)


def place():
    d, t = lax.axis_index("dp"), lax.axis_index("tensor")
    return d >> 1, d & 1, t >> 1, t & 1


def shape(rows, columns, kind=BF16):
    return jax.ShapeDtypeStruct((rows, columns), kind)


VMEM = pl.BlockSpec(memory_space=pltpu.VMEM)
HBM = pl.BlockSpec(memory_space=pltpu.HBM)
ANY = pl.BlockSpec(memory_space=pl.ANY)


def call(name, kernel, operands, out_shape, behind=(), specs=None, scratch=(), flops=0, limit=16, weigh=1):
    specs = specs or [VMEM] * len(operands)
    count = len(operands)
    outs = out_shape if isinstance(out_shape, tuple) else (out_shape,)
    size = sum(2 * math.prod(o.shape) for o in tuple(operands) + outs)
    return pl.pallas_call(
        lambda *refs: kernel(*refs[:count], *refs[count + len(behind) :]),
        out_shape=out_shape,
        in_specs=list(specs) + [ANY] * len(behind),
        out_specs=jax.tree.map(lambda _: VMEM, out_shape),
        scratch_shapes=list(scratch),
        compiler_params=pltpu.CompilerParams(vmem_limit_bytes=limit << 20),
        cost_estimate=pl.CostEstimate(flops=flops, bytes_accessed=size * weigh, transcendentals=0),
        name=name,
    )(*operands, *behind)


def rotate_kernel(scale, x_ref, s_ref, o_ref):
    rows, width = o_ref.shape
    pieces = width // LANES
    signs = f32(s_ref[...])
    i = lax.broadcasted_iota(jnp.int32, (LANES, LANES), 0) & lax.broadcasted_iota(jnp.int32, (LANES, LANES), 1)
    for bits in (4, 2, 1):
        i = i ^ (i >> bits)
    table = f32(1 - 2 * (i & 1)).astype(BF16)
    for r in range(0, rows, 32):
        part = []
        for a in range(pieces):
            cols = slice(a * LANES, (a + 1) * LANES)
            x = (f32(x_ref[0, r : r + 32, cols]) * signs[:, cols]).astype(BF16)
            part.append(jnp.dot(x, table, preferred_element_type=jnp.float32))
        step = 1
        while step < pieces:
            nxt = list(part)
            for a in range(pieces):
                if not a & step:
                    nxt[a] = part[a] + part[a | step]
                    nxt[a | step] = part[a] - part[a | step]
            part = nxt
            step *= 2
        for a in range(pieces):
            o_ref[r : r + 32, a * LANES : (a + 1) * LANES] = (part[a] * scale).astype(BF16)


def pair_kernel(at, mine_ref, other_ref, out_ref):
    sign = f32(1 - 2 * place()[3])
    out_ref[...] = (f32(other_ref[at]) + sign * f32(mine_ref[at])).astype(BF16)


def mix_kernel(*refs):
    z = place()[2]
    total = 0
    for k, ref in enumerate(refs[:4]):
        u = z & ((z + k) & 3)
        total = total + f32(1 - 2 * ((u ^ (u >> 1)) & 1)) * f32(ref[...])
    refs[4][...] = total.astype(BF16)


def load_kernel(w_ref, out_ref, sem):
    copy = pltpu.make_async_copy(w_ref.at[0], out_ref, sem)
    copy.start()
    copy.wait()


def products(blocks, w_ref, lhs, store):
    width = w_ref.shape[1] // TILES
    y, _, z, _ = place()
    rows = blocks[0].shape[0]
    for dy, ref in enumerate(blocks):
        lhs[pl.ds(pl.multiple_of(((y + dy - z) & 3) * rows, rows), rows), :] = ref[...]
    for n in range(TILES):
        cols = slice(n * width, (n + 1) * width)
        out = jnp.dot(lhs[...], w_ref[:, cols], preferred_element_type=jnp.float32)
        store(cols, out.astype(BF16))


def column_kernel(*refs):
    blocks, (w_ref, out_ref, lhs) = refs[:4], refs[4:]

    def store(cols, out):
        out_ref[:, cols] = out

    products(blocks, w_ref, lhs, store)


def mate_kernel(*refs):
    blocks, (w_ref, column_ref, keep_ref, send_ref, lhs) = refs[:4], refs[4:]
    _, x, _, c = place()

    def store(cols, out):
        @pl.when(x == c)
        def _():
            keep_ref[:, cols] = column_ref[:, cols]
            send_ref[:, cols] = out

        @pl.when(x != c)
        def _():
            keep_ref[:, cols] = out
            send_ref[:, cols] = column_ref[:, cols]

    products(blocks, w_ref, lhs, store)


def project(blocks, weight, column=None, behind=()):
    rows, depth = blocks[0].shape
    width = weight.shape[1]
    half = shape(4 * rows, width)
    return call(
        "project_column" if column is None else "project_mate",
        column_kernel if column is None else mate_kernel,
        (*blocks, weight) + (() if column is None else (column,)),
        half if column is None else (half, half),
        behind,
        scratch=[pltpu.VMEM((4 * rows, depth), BF16)],
        flops=2 * 4 * rows * depth * width,
        limit=24,
    )


def halves_kernel(keep_ref, came_ref, *out_refs):
    rows = out_refs[0].shape[0]
    for k, ref in enumerate(out_refs, 1):
        at = slice(k * rows, (k + 1) * rows)
        ref[...] = (f32(keep_ref[at]) + f32(came_ref[at])).astype(BF16)


def finish_kernel(at, keep_ref, came_ref, a_ref, b_ref, c_ref, residual_ref, leading_ref, summed_ref):
    rows = leading_ref.shape[0]
    total = f32(keep_ref[:rows]) + f32(came_ref[:rows]) + f32(a_ref[...]) + f32(b_ref[...]) + f32(c_ref[...])
    summed_ref[...] = total
    leading_ref[...] = (f32(residual_ref[at]) + total).astype(BF16)


def end_kernel(*refs):
    out_ref = refs[-1]
    first = lax.axis_index("pipe") == 0
    at = 0
    for leading_ref, summed_ref, passed_ref in zip(refs[0:-1:3], refs[1:-1:3], refs[2:-1:3]):
        rows = leading_ref.shape[0]
        later = (f32(passed_ref[...]) + summed_ref[...]).astype(BF16)
        out_ref[0, at : at + rows, :] = jnp.where(first, leading_ref[...], later)
        at += rows


def on_device(attention_out, signs, out_weight, residual_in):
    tokens, width = attention_out.shape[1:]
    columns = out_weight.shape[2]
    scale = 1.0 / math.sqrt(width * lax.axis_size("tensor"))
    rows = tokens // 2
    cut = [slice(0, rows), slice(rows, tokens)]

    def move(value, axis, target):
        return lax.ppermute(value, axis, [(i, target(i)) for i in range(lax.axis_size(axis))])

    def ring(steps, flip=0):
        return lambda i: (i // 2 + steps) % 4 * 2 + (i % 2 ^ flip)

    def swap(value):
        return move(value, "tensor", lambda i: i ^ 1)

    def pipe(value):
        return lax.ppermute(value, "pipe", [(0, 1)])

    def pair(chunk, mine, other, behind=()):
        return call(
            "hadamard_core", lambda *refs: pair_kernel(cut[chunk], *refs), (mine, other), shape(rows, width), behind
        )

    def spread_z(mine):
        return [mine] + [move(mine, "tensor", ring(-k)) for k in (1, 2, 3)]

    def mix(terms, behind=()):
        return call("hadamard_z", mix_kernel, terms, shape(rows, width), behind)

    def spread_column(own):
        mate = move(own, "dp", ring(0, 1))
        return [own] + [move(own, "dp", ring(-dy)) for dy in (1, 2, 3)], mate

    def spread_mate(column, mate):
        return [mate, move(mate, "dp", ring(-1)), move(column[2], "dp", ring(0, 1)), move(mate, "dp", ring(-3))]

    def halves(keep, came, behind=()):
        return call("core_sum", halves_kernel, (keep, came), (shape(rows, columns),) * 3, behind)

    def gather_z(parts):
        return [move(part, "tensor", ring(k)) for k, part in enumerate(parts, 1)]

    def finish(chunk, keep, came, arrived, behind=()):
        return call(
            "residual",
            lambda *refs: finish_kernel(cut[chunk], *refs),
            (keep, came, *arrived, residual_in),
            (shape(rows, columns), shape(rows, columns, jnp.float32)),
            behind,
            weigh=20,
        )

    local = call(
        "rotate_local",
        lambda *refs: rotate_kernel(scale, *refs),
        (attention_out, signs),
        shape(tokens, width),
        flops=2 * tokens * width * LANES,
    )
    other = swap(local)
    terms0 = spread_z(pair(0, local, other))
    terms1 = spread_z(pair(1, local, other, [terms0[1]]))
    weight = call(
        "load_weight",
        load_kernel,
        (out_weight,),
        shape(*out_weight.shape[1:]),
        [terms0[0]],
        specs=[HBM],
        scratch=[pltpu.SemaphoreType.DMA],
        limit=48,
    )
    own0 = mix(terms0, [weight])
    own1 = mix(terms1, [own0])
    column0, mate0 = spread_column(own0)
    column1, mate1 = spread_column(own1)
    mates0 = spread_mate(column0, mate0)
    products0 = project(column0, weight, None, [own1])
    keep0, send0 = project(mates0, weight, products0, [*column1[1:], mate1])
    came0 = swap(send0)
    mates1 = spread_mate(column1, mate1)
    products1 = project(column1, weight, None, [send0])
    parts0 = halves(keep0, came0, [products1])
    arrived0 = gather_z(parts0)
    keep1, send1 = project(mates1, weight, products1, [parts0[0]])
    came1 = swap(send1)
    leading0, summed0 = finish(0, keep0, came0, arrived0, [send1])
    passed0 = pipe(leading0)
    parts1 = halves(keep1, came1, [leading0])
    arrived1 = gather_z(parts1)
    leading1, summed1 = finish(1, keep1, came1, arrived1)
    passed1 = pipe(leading1)
    return call(
        "end",
        end_kernel,
        (leading0, summed0, passed0, leading1, summed1, passed1),
        jax.ShapeDtypeStruct((1, tokens, columns), BF16),
    )


def solution(mesh):
    in_specs = (
        P("pipe", "dp", "tensor"),
        P("pipe", "tensor"),
        P("pipe", "tensor", "dp"),
        P("tensor", "dp"),
    )
    out_specs = P("pipe", "tensor", "dp")
    return jax.shard_map(
        on_device, mesh=mesh, in_specs=in_specs, out_specs=out_specs, check_vma=False
    )
```

```python
import math

import jax
import jax.numpy as jnp
from jax import lax
from jax.experimental import pallas as pl
from jax.experimental.pallas import tpu as pltpu
from jax.sharding import PartitionSpec as P

LANES = 128
BF16 = jnp.bfloat16
TILES = 4


def f32(value):
    return value.astype(jnp.float32)


def place():
    d, t = lax.axis_index("dp"), lax.axis_index("tensor")
    return d >> 1, d & 1, t >> 1, t & 1


def shape(rows, columns, kind=BF16):
    return jax.ShapeDtypeStruct((rows, columns), kind)


VMEM = pl.BlockSpec(memory_space=pltpu.VMEM)
HBM = pl.BlockSpec(memory_space=pltpu.HBM)
ANY = pl.BlockSpec(memory_space=pl.ANY)


def call(name, kernel, operands, out_shape, behind=(), specs=None, scratch=(), flops=0, limit=16, weigh=1):
    specs = specs or [VMEM] * len(operands)
    count = len(operands)
    outs = out_shape if isinstance(out_shape, tuple) else (out_shape,)
    size = sum(2 * math.prod(o.shape) for o in tuple(operands) + outs)
    return pl.pallas_call(
        lambda *refs: kernel(*refs[:count], *refs[count + len(behind) :]),
        out_shape=out_shape,
        in_specs=list(specs) + [ANY] * len(behind),
        out_specs=jax.tree.map(lambda _: VMEM, out_shape),
        scratch_shapes=list(scratch),
        compiler_params=pltpu.CompilerParams(vmem_limit_bytes=limit << 20),
        cost_estimate=pl.CostEstimate(flops=flops * weigh, bytes_accessed=size * weigh, transcendentals=0),
        name=name,
    )(*operands, *behind)


def rotate_kernel(scale, x_ref, s_ref, o_ref):
    rows, width = o_ref.shape
    pieces = width // LANES
    signs = f32(s_ref[...])
    i = lax.broadcasted_iota(jnp.int32, (LANES, LANES), 0) & lax.broadcasted_iota(jnp.int32, (LANES, LANES), 1)
    for bits in (4, 2, 1):
        i = i ^ (i >> bits)
    table = f32(1 - 2 * (i & 1)).astype(BF16)
    for r in range(0, rows, 32):
        part = []
        for a in range(pieces):
            cols = slice(a * LANES, (a + 1) * LANES)
            x = (f32(x_ref[0, r : r + 32, cols]) * signs[:, cols]).astype(BF16)
            part.append(jnp.dot(x, table, preferred_element_type=jnp.float32))
        step = 1
        while step < pieces:
            nxt = list(part)
            for a in range(pieces):
                if not a & step:
                    nxt[a] = part[a] + part[a | step]
                    nxt[a | step] = part[a] - part[a | step]
            part = nxt
            step *= 2
        for a in range(pieces):
            o_ref[r : r + 32, a * LANES : (a + 1) * LANES] = (part[a] * scale).astype(BF16)


def pair_kernel(at, mine_ref, other_ref, out_ref):
    sign = f32(1 - 2 * place()[3])
    out_ref[...] = (f32(other_ref[at]) + sign * f32(mine_ref[at])).astype(BF16)


def mix_kernel(*refs):
    z = place()[2]
    total = 0
    for k, ref in enumerate(refs[:4]):
        u = z & ((z + k) & 3)
        total = total + f32(1 - 2 * ((u ^ (u >> 1)) & 1)) * f32(ref[...])
    refs[4][...] = total.astype(BF16)


def touch_kernel(w_ref, out_ref):
    out_ref[...] = jnp.zeros_like(out_ref)


def products(blocks, w_ref, lhs, store):
    width = w_ref.shape[2] // TILES
    y, _, z, _ = place()
    rows = blocks[0].shape[0]
    for dy, ref in enumerate(blocks):
        lhs[pl.ds(pl.multiple_of(((y + dy - z) & 3) * rows, rows), rows), :] = ref[...]
    for n in range(TILES):
        cols = slice(n * width, (n + 1) * width)
        out = jnp.dot(lhs[...], w_ref[0, :, cols], preferred_element_type=jnp.float32)
        store(cols, out.astype(BF16))


def column_kernel(*refs):
    blocks, (w_ref, out_ref, lhs) = refs[:4], refs[4:]

    def store(cols, out):
        out_ref[:, cols] = out

    products(blocks, w_ref, lhs, store)


def mate_kernel(*refs):
    blocks, (w_ref, column_ref, keep_ref, send_ref, lhs) = refs[:4], refs[4:]
    _, x, _, c = place()

    def store(cols, out):
        @pl.when(x == c)
        def _():
            keep_ref[:, cols] = column_ref[:, cols]
            send_ref[:, cols] = out

        @pl.when(x != c)
        def _():
            keep_ref[:, cols] = out
            send_ref[:, cols] = column_ref[:, cols]

    products(blocks, w_ref, lhs, store)


def project(blocks, weight, column=None, behind=()):
    rows, depth = blocks[0].shape
    width = weight.shape[2]
    half = shape(4 * rows, width)
    return call(
        "project_column" if column is None else "project_mate",
        column_kernel if column is None else mate_kernel,
        (*blocks, weight) + (() if column is None else (column,)),
        half if column is None else (half, half),
        behind,
        scratch=[pltpu.VMEM((4 * rows, depth), BF16)],
        flops=2 * 4 * rows * depth * width,
        weigh=5,
        limit=24,
    )


def halves_kernel(keep_ref, came_ref, *out_refs):
    rows = out_refs[0].shape[0]
    for k, ref in enumerate(out_refs, 1):
        at = slice(k * rows, (k + 1) * rows)
        ref[...] = (f32(keep_ref[at]) + f32(came_ref[at])).astype(BF16)


def finish_kernel(at, keep_ref, came_ref, a_ref, b_ref, c_ref, residual_ref, leading_ref, summed_ref):
    rows = leading_ref.shape[0]
    total = f32(keep_ref[:rows]) + f32(came_ref[:rows]) + f32(a_ref[...]) + f32(b_ref[...]) + f32(c_ref[...])
    summed_ref[...] = total
    leading_ref[...] = (f32(residual_ref[at]) + total).astype(BF16)


def end_kernel(*refs):
    out_ref = refs[-1]
    first = lax.axis_index("pipe") == 0
    at = 0
    for leading_ref, summed_ref, passed_ref in zip(refs[0:-1:3], refs[1:-1:3], refs[2:-1:3]):
        rows = leading_ref.shape[0]
        later = (f32(passed_ref[...]) + summed_ref[...]).astype(BF16)
        out_ref[0, at : at + rows, :] = jnp.where(first, leading_ref[...], later)
        at += rows


def on_device(attention_out, signs, out_weight, residual_in):
    tokens, width = attention_out.shape[1:]
    columns = out_weight.shape[2]
    scale = 1.0 / math.sqrt(width * lax.axis_size("tensor"))
    rows = tokens // 2
    cut = [slice(0, rows), slice(rows, tokens)]

    def move(value, axis, target):
        return lax.ppermute(value, axis, [(i, target(i)) for i in range(lax.axis_size(axis))])

    def ring(steps, flip=0):
        return lambda i: (i // 2 + steps) % 4 * 2 + (i % 2 ^ flip)

    def swap(value):
        return move(value, "tensor", lambda i: i ^ 1)

    def pipe(value):
        return lax.ppermute(value, "pipe", [(0, 1)])

    def pair(chunk, mine, other, behind=()):
        return call(
            "hadamard_core", lambda *refs: pair_kernel(cut[chunk], *refs), (mine, other), shape(rows, width), behind
        )

    def spread_z(mine):
        return [mine] + [move(mine, "tensor", ring(-k)) for k in (1, 2, 3)]

    def mix(terms, behind=()):
        return call("hadamard_z", mix_kernel, terms, shape(rows, width), behind, weigh=20)

    def spread_column(own):
        mate = move(own, "dp", ring(0, 1))
        return [own] + [move(own, "dp", ring(-dy)) for dy in (1, 2, 3)], mate

    def spread_mate(column, mate):
        return [mate, move(mate, "dp", ring(-1)), move(column[2], "dp", ring(0, 1)), move(mate, "dp", ring(-3))]

    def halves(keep, came, behind=()):
        return call("core_sum", halves_kernel, (keep, came), (shape(rows, columns),) * 3, behind)

    def gather_z(parts):
        return [move(part, "tensor", ring(k)) for k, part in enumerate(parts, 1)]

    def finish(chunk, keep, came, arrived, behind=()):
        return call(
            "residual",
            lambda *refs: finish_kernel(cut[chunk], *refs),
            (keep, came, *arrived, residual_in),
            (shape(rows, columns), shape(rows, columns, jnp.float32)),
            behind,
            weigh=20,
        )

    local = call(
        "rotate_local",
        lambda *refs: rotate_kernel(scale, *refs),
        (attention_out, signs),
        shape(tokens, width),
        flops=2 * tokens * width * LANES,
    )
    other = swap(local)
    terms0 = spread_z(pair(0, local, other))
    ready = call("weight", touch_kernel, (out_weight,), shape(8, LANES), [terms0[0]], weigh=9)
    terms1 = spread_z(pair(1, local, other, [terms0[1], ready]))
    own0 = mix(terms0, [terms1[0]])
    column0, mate0 = spread_column(own0)
    own1 = mix(terms1, [mate0, column0[2]])
    mates0 = spread_mate(column0, mate0)
    column1, mate1 = spread_column(own1)
    products0 = project(column0, out_weight, None, [own1])
    keep0, send0 = project(mates0, out_weight, products0)
    came0 = swap(send0)
    mates1 = spread_mate(column1, mate1)
    products1 = project(column1, out_weight, None, [send0])
    parts0 = halves(keep0, came0, [products1])
    arrived0 = gather_z(parts0)
    keep1, send1 = project(mates1, out_weight, products1, [parts0[0]])
    came1 = swap(send1)
    leading0, summed0 = finish(0, keep0, came0, arrived0, [send1])
    passed0 = pipe(leading0)
    parts1 = halves(keep1, came1, [leading0])
    arrived1 = gather_z(parts1)
    leading1, summed1 = finish(1, keep1, came1, arrived1)
    passed1 = pipe(leading1)
    return call(
        "end",
        end_kernel,
        (leading0, summed0, passed0, leading1, summed1, passed1),
        jax.ShapeDtypeStruct((1, tokens, columns), BF16),
    )


def solution(mesh):
    in_specs = (
        P("pipe", "dp", "tensor"),
        P("pipe", "tensor"),
        P("pipe", "tensor", "dp"),
        P("tensor", "dp"),
    )
    out_specs = P("pipe", "tensor", "dp")
    return jax.shard_map(
        on_device, mesh=mesh, in_specs=in_specs, out_specs=out_specs, check_vma=False
    )
```

```python
import math

import jax
import jax.numpy as jnp
from jax import lax
from jax.experimental import pallas as pl
from jax.experimental.pallas import tpu as pltpu
from jax.sharding import PartitionSpec as P

LANES = 128
BF16 = jnp.bfloat16
TILES = 4


def f32(value):
    return value.astype(jnp.float32)


def place():
    d, t = lax.axis_index("dp"), lax.axis_index("tensor")
    return d >> 1, d & 1, t >> 1, t & 1


def shape(rows, columns, kind=BF16):
    return jax.ShapeDtypeStruct((rows, columns), kind)


VMEM = pl.BlockSpec(memory_space=pltpu.VMEM)
HBM = pl.BlockSpec(memory_space=pltpu.HBM)
ANY = pl.BlockSpec(memory_space=pl.ANY)


def call(name, kernel, operands, out_shape, behind=(), specs=None, scratch=(), flops=0, limit=16, weigh=1):
    specs = specs or [VMEM] * len(operands)
    count = len(operands)
    outs = out_shape if isinstance(out_shape, tuple) else (out_shape,)
    size = sum(2 * math.prod(o.shape) for o in tuple(operands) + outs)
    return pl.pallas_call(
        lambda *refs: kernel(*refs[:count], *refs[count + len(behind) :]),
        out_shape=out_shape,
        in_specs=list(specs) + [ANY] * len(behind),
        out_specs=jax.tree.map(lambda _: VMEM, out_shape),
        scratch_shapes=list(scratch),
        compiler_params=pltpu.CompilerParams(vmem_limit_bytes=limit << 20),
        cost_estimate=pl.CostEstimate(flops=flops * weigh, bytes_accessed=size * weigh, transcendentals=0),
        name=name,
    )(*operands, *behind)


def rotate_kernel(scale, x_ref, s_ref, o_ref):
    rows, width = o_ref.shape
    pieces = width // LANES
    signs = f32(s_ref[...])
    i = lax.broadcasted_iota(jnp.int32, (LANES, LANES), 0) & lax.broadcasted_iota(jnp.int32, (LANES, LANES), 1)
    for bits in (4, 2, 1):
        i = i ^ (i >> bits)
    table = f32(1 - 2 * (i & 1)).astype(BF16)
    for r in range(0, rows, 32):
        part = []
        for a in range(pieces):
            cols = slice(a * LANES, (a + 1) * LANES)
            x = (f32(x_ref[0, r : r + 32, cols]) * signs[:, cols]).astype(BF16)
            part.append(jnp.dot(x, table, preferred_element_type=jnp.float32))
        step = 1
        while step < pieces:
            nxt = list(part)
            for a in range(pieces):
                if not a & step:
                    nxt[a] = part[a] + part[a | step]
                    nxt[a | step] = part[a] - part[a | step]
            part = nxt
            step *= 2
        for a in range(pieces):
            o_ref[r : r + 32, a * LANES : (a + 1) * LANES] = (part[a] * scale).astype(BF16)


def pair_kernel(at, mine_ref, other_ref, out_ref):
    sign = f32(1 - 2 * place()[3])
    out_ref[...] = (f32(other_ref[at]) + sign * f32(mine_ref[at])).astype(BF16)


def mix_kernel(mine_ref, next_ref, last_ref, low_ref, high_ref, out_ref):
    z = place()[2]
    half = low_ref.shape[0]

    def sign(k):
        u = z & ((z + k) & 3)
        return f32(1 - 2 * ((u ^ (u >> 1)) & 1))

    for at, far_ref in ((slice(0, half), low_ref), (slice(half, 2 * half), high_ref)):
        total = sign(0) * f32(mine_ref[at]) + sign(1) * f32(next_ref[at]) + sign(3) * f32(last_ref[at])
        out_ref[at] = (total + sign(2) * f32(far_ref[...])).astype(BF16)


def touch_kernel(w_ref, out_ref):
    out_ref[...] = jnp.zeros_like(out_ref)


def products(blocks, w_ref, lhs, store):
    width = w_ref.shape[2] // TILES
    y, _, z, _ = place()
    rows = blocks[0].shape[0]
    for dy, ref in enumerate(blocks):
        lhs[pl.ds(pl.multiple_of(((y + dy - z) & 3) * rows, rows), rows), :] = ref[...]
    for n in range(TILES):
        cols = slice(n * width, (n + 1) * width)
        out = jnp.dot(lhs[...], w_ref[0, :, cols], preferred_element_type=jnp.float32)
        store(cols, out.astype(BF16))


def column_kernel(*refs):
    blocks, (w_ref, out_ref, lhs) = refs[:4], refs[4:]

    def store(cols, out):
        out_ref[:, cols] = out

    products(blocks, w_ref, lhs, store)


def mate_kernel(*refs):
    blocks, (w_ref, column_ref, keep_ref, send_ref, lhs) = refs[:4], refs[4:]
    _, x, _, c = place()

    def store(cols, out):
        @pl.when(x == c)
        def _():
            keep_ref[:, cols] = column_ref[:, cols]
            send_ref[:, cols] = out

        @pl.when(x != c)
        def _():
            keep_ref[:, cols] = out
            send_ref[:, cols] = column_ref[:, cols]

    products(blocks, w_ref, lhs, store)


def project(blocks, weight, column=None, behind=()):
    rows, depth = blocks[0].shape
    width = weight.shape[2]
    half = shape(4 * rows, width)
    return call(
        "project_column" if column is None else "project_mate",
        column_kernel if column is None else mate_kernel,
        (*blocks, weight) + (() if column is None else (column,)),
        half if column is None else (half, half),
        behind,
        scratch=[pltpu.VMEM((4 * rows, depth), BF16)],
        flops=2 * 4 * rows * depth * width,
        weigh=5,
        limit=24,
    )


def core_sum(keep_ref, came_ref, k, low=0, high=None):
    rows = keep_ref.shape[0] // 4
    at = slice(k * rows + low, k * rows + (high or rows))
    return f32(keep_ref[at]) + f32(came_ref[at])


def far_kernel(keep_ref, came_ref, low_ref, high_ref):
    half = low_ref.shape[0]
    low_ref[...] = core_sum(keep_ref, came_ref, 2, 0, half).astype(BF16)
    high_ref[...] = core_sum(keep_ref, came_ref, 2, half).astype(BF16)


def near_kernel(keep_ref, came_ref, low_ref, high_ref, next_ref, last_ref):
    half = low_ref.shape[0]
    next_ref[:half] = (core_sum(keep_ref, came_ref, 1, 0, half) + f32(low_ref[...])).astype(BF16)
    next_ref[half:] = core_sum(keep_ref, came_ref, 1, half).astype(BF16)
    last_ref[:half] = core_sum(keep_ref, came_ref, 3, 0, half).astype(BF16)
    last_ref[half:] = (core_sum(keep_ref, came_ref, 3, half) + f32(high_ref[...])).astype(BF16)


def finish_kernel(at, keep_ref, came_ref, a_ref, b_ref, residual_ref, leading_ref, summed_ref):
    total = core_sum(keep_ref, came_ref, 0) + f32(a_ref[...]) + f32(b_ref[...])
    summed_ref[...] = total
    leading_ref[...] = (f32(residual_ref[at]) + total).astype(BF16)


def end_kernel(*refs):
    out_ref = refs[-1]
    first = lax.axis_index("pipe") == 0
    at = 0
    for leading_ref, summed_ref, passed_ref in zip(refs[0:-1:3], refs[1:-1:3], refs[2:-1:3]):
        rows = leading_ref.shape[0]
        later = (f32(passed_ref[...]) + summed_ref[...]).astype(BF16)
        out_ref[0, at : at + rows, :] = jnp.where(first, leading_ref[...], later)
        at += rows


def on_device(attention_out, signs, out_weight, residual_in):
    tokens, width = attention_out.shape[1:]
    columns = out_weight.shape[2]
    scale = 1.0 / math.sqrt(width * lax.axis_size("tensor"))
    rows = tokens // 2
    cut = [slice(0, rows), slice(rows, tokens)]

    def move(value, axis, target):
        return lax.ppermute(value, axis, [(i, target(i)) for i in range(lax.axis_size(axis))])

    def ring(steps, flip=0):
        return lambda i: (i // 2 + steps) % 4 * 2 + (i % 2 ^ flip)

    def swap(value):
        return move(value, "tensor", lambda i: i ^ 1)

    def pipe(value):
        return lax.ppermute(value, "pipe", [(0, 1)])

    def pair(chunk, mine, other, behind=()):
        return call(
            "hadamard_core", lambda *refs: pair_kernel(cut[chunk], *refs), (mine, other), shape(rows, width), behind
        )

    half = rows // 2

    def up(value):
        return move(value, "tensor", ring(1))

    def down(value):
        return move(value, "tensor", ring(-1))

    def near_z(mine):
        return [mine, down(mine), up(mine)]

    def far_z(terms):
        return terms + [up(terms[2][:half]), down(terms[1][half:])]

    def mix(terms, behind=()):
        return call("hadamard_z", mix_kernel, terms, shape(rows, width), behind, weigh=20)

    def spread_column(own):
        mate = move(own, "dp", ring(0, 1))
        return [own] + [move(own, "dp", ring(-dy)) for dy in (1, 2, 3)], mate

    def spread_mate(column, mate):
        return [mate, move(mate, "dp", ring(-1)), move(column[2], "dp", ring(0, 1)), move(mate, "dp", ring(-3))]

    def far_sum(keep, came, behind=()):
        low, high = call("far_sum", far_kernel, (keep, came), (shape(half, columns),) * 2, behind)
        return up(low), down(high)

    def near_sum(keep, came, far, behind=()):
        return call("near_sum", near_kernel, (keep, came, *far), (shape(rows, columns),) * 2, behind)

    def last_sum(near):
        return up(near[0]), down(near[1])

    def finish(chunk, keep, came, arrived, behind=()):
        return call(
            "residual",
            lambda *refs: finish_kernel(cut[chunk], *refs),
            (keep, came, *arrived, residual_in),
            (shape(rows, columns), shape(rows, columns, jnp.float32)),
            behind,
            weigh=20,
        )

    local = call(
        "rotate_local",
        lambda *refs: rotate_kernel(scale, *refs),
        (attention_out, signs),
        shape(tokens, width),
        flops=2 * tokens * width * LANES,
    )
    other = swap(local)
    terms0 = near_z(pair(0, local, other))
    ready = call("weight", touch_kernel, (out_weight,), shape(8, LANES), [terms0[0]], weigh=9)
    terms1 = near_z(pair(1, local, other, [terms0[1], ready]))
    own0 = mix(far_z(terms0), [terms1[0]])
    column0, mate0 = spread_column(own0)
    mates0 = spread_mate(column0, mate0)
    own1 = mix(far_z(terms1), [mates0[1], mates0[3]])
    column1, mate1 = spread_column(own1)
    products0 = project(column0, out_weight, None, [own1])
    keep0, send0 = project(mates0, out_weight, products0, [mate1, column1[1], column1[3]])
    came0 = swap(send0)
    mates1 = spread_mate(column1, mate1)
    far0 = far_sum(keep0, came0)
    products1 = project(column1, out_weight, None, [far0[0]])
    near0 = near_sum(keep0, came0, far0)
    keep1, send1 = project(mates1, out_weight, products1, [near0[0]])
    came1 = swap(send1)
    far1 = far_sum(keep1, came1)
    leading0, summed0 = finish(0, keep0, came0, last_sum(near0), [far1[0]])
    passed0 = pipe(leading0)
    near1 = near_sum(keep1, came1, far1)
    leading1, summed1 = finish(1, keep1, came1, last_sum(near1), [leading0])
    passed1 = pipe(leading1)
    return call(
        "end",
        end_kernel,
        (leading0, summed0, passed0, leading1, summed1, passed1),
        jax.ShapeDtypeStruct((1, tokens, columns), BF16),
    )


def solution(mesh):
    in_specs = (
        P("pipe", "dp", "tensor"),
        P("pipe", "tensor"),
        P("pipe", "tensor", "dp"),
        P("tensor", "dp"),
    )
    out_specs = P("pipe", "tensor", "dp")
    return jax.shard_map(
        on_device, mesh=mesh, in_specs=in_specs, out_specs=out_specs, check_vma=False
    )
```

```python
import math

import jax
import jax.numpy as jnp
from jax import lax
from jax.experimental import pallas as pl
from jax.experimental.pallas import tpu as pltpu
from jax.sharding import PartitionSpec as P

LANES = 128
BF16 = jnp.bfloat16
TILES = 4


def f32(value):
    return value.astype(jnp.float32)


def place():
    d, t = lax.axis_index("dp"), lax.axis_index("tensor")
    return d >> 1, d & 1, t >> 1, t & 1


def shape(rows, columns, kind=BF16):
    return jax.ShapeDtypeStruct((rows, columns), kind)


VMEM = pl.BlockSpec(memory_space=pltpu.VMEM)
HBM = pl.BlockSpec(memory_space=pltpu.HBM)
ANY = pl.BlockSpec(memory_space=pl.ANY)


def call(name, kernel, operands, out_shape, behind=(), specs=None, scratch=(), flops=0, limit=16, weigh=1):
    specs = specs or [VMEM] * len(operands)
    count = len(operands)
    outs = out_shape if isinstance(out_shape, tuple) else (out_shape,)
    size = sum(2 * math.prod(o.shape) for o in tuple(operands) + outs)
    return pl.pallas_call(
        lambda *refs: kernel(*refs[:count], *refs[count + len(behind) :]),
        out_shape=out_shape,
        in_specs=list(specs) + [ANY] * len(behind),
        out_specs=jax.tree.map(lambda _: VMEM, out_shape),
        scratch_shapes=list(scratch),
        compiler_params=pltpu.CompilerParams(vmem_limit_bytes=limit << 20),
        cost_estimate=pl.CostEstimate(flops=flops * weigh, bytes_accessed=size * weigh, transcendentals=0),
        name=name,
    )(*operands, *behind)


def rotate_kernel(scale, x_ref, s_ref, o_ref):
    rows, width = o_ref.shape
    pieces = width // LANES
    signs = f32(s_ref[...])
    i = lax.broadcasted_iota(jnp.int32, (LANES, LANES), 0) & lax.broadcasted_iota(jnp.int32, (LANES, LANES), 1)
    for bits in (4, 2, 1):
        i = i ^ (i >> bits)
    table = f32(1 - 2 * (i & 1)).astype(BF16)
    for r in range(0, rows, 32):
        part = []
        for a in range(pieces):
            cols = slice(a * LANES, (a + 1) * LANES)
            x = (f32(x_ref[0, r : r + 32, cols]) * signs[:, cols]).astype(BF16)
            part.append(jnp.dot(x, table, preferred_element_type=jnp.float32))
        step = 1
        while step < pieces:
            nxt = list(part)
            for a in range(pieces):
                if not a & step:
                    nxt[a] = part[a] + part[a | step]
                    nxt[a | step] = part[a] - part[a | step]
            part = nxt
            step *= 2
        for a in range(pieces):
            o_ref[r : r + 32, a * LANES : (a + 1) * LANES] = (part[a] * scale).astype(BF16)


def pair_kernel(at, mine_ref, other_ref, out_ref):
    sign = f32(1 - 2 * place()[3])
    out_ref[...] = (f32(other_ref[at]) + sign * f32(mine_ref[at])).astype(BF16)


def cut_kernel(next_ref, last_ref, low_ref, high_ref):
    half = low_ref.shape[0]
    low_ref[...] = last_ref[:half]
    high_ref[...] = next_ref[half:]


def mix_kernel(mine_ref, next_ref, last_ref, low_ref, high_ref, out_ref):
    z = place()[2]
    half = low_ref.shape[0]

    def sign(k):
        u = z & ((z + k) & 3)
        return f32(1 - 2 * ((u ^ (u >> 1)) & 1))

    for at, far_ref in ((slice(0, half), low_ref), (slice(half, 2 * half), high_ref)):
        total = sign(0) * f32(mine_ref[at]) + sign(1) * f32(next_ref[at]) + sign(3) * f32(last_ref[at])
        out_ref[at] = (total + sign(2) * f32(far_ref[...])).astype(BF16)


def touch_kernel(w_ref, out_ref):
    out_ref[...] = jnp.zeros_like(out_ref)


def products(blocks, w_ref, lhs, store):
    width = w_ref.shape[2] // TILES
    y, _, z, _ = place()
    rows = blocks[0].shape[0]
    for dy, ref in enumerate(blocks):
        lhs[pl.ds(pl.multiple_of(((y + dy - z) & 3) * rows, rows), rows), :] = ref[...]
    for n in range(TILES):
        cols = slice(n * width, (n + 1) * width)
        out = jnp.dot(lhs[...], w_ref[0, :, cols], preferred_element_type=jnp.float32)
        store(cols, out.astype(BF16))


def column_kernel(*refs):
    blocks, (w_ref, out_ref, lhs) = refs[:4], refs[4:]

    def store(cols, out):
        out_ref[:, cols] = out

    products(blocks, w_ref, lhs, store)


def mate_kernel(*refs):
    blocks, (w_ref, column_ref, keep_ref, send_ref, lhs) = refs[:4], refs[4:]
    _, x, _, c = place()

    def store(cols, out):
        @pl.when(x == c)
        def _():
            keep_ref[:, cols] = column_ref[:, cols]
            send_ref[:, cols] = out

        @pl.when(x != c)
        def _():
            keep_ref[:, cols] = out
            send_ref[:, cols] = column_ref[:, cols]

    products(blocks, w_ref, lhs, store)


def project(blocks, weight, column=None, behind=()):
    rows, depth = blocks[0].shape
    width = weight.shape[2]
    half = shape(4 * rows, width)
    return call(
        "project_column" if column is None else "project_mate",
        column_kernel if column is None else mate_kernel,
        (*blocks, weight) + (() if column is None else (column,)),
        half if column is None else (half, half),
        behind,
        scratch=[pltpu.VMEM((4 * rows, depth), BF16)],
        flops=2 * 4 * rows * depth * width,
        weigh=5,
        limit=24,
    )


def core_sum(keep_ref, came_ref, k, low=0, high=None):
    rows = keep_ref.shape[0] // 4
    at = slice(k * rows + low, k * rows + (high or rows))
    return f32(keep_ref[at]) + f32(came_ref[at])


def far_kernel(keep_ref, came_ref, low_ref, high_ref):
    half = low_ref.shape[0]
    low_ref[...] = core_sum(keep_ref, came_ref, 2, 0, half).astype(BF16)
    high_ref[...] = core_sum(keep_ref, came_ref, 2, half).astype(BF16)


def near_kernel(keep_ref, came_ref, low_ref, high_ref, next_ref, last_ref):
    half = low_ref.shape[0]
    next_ref[:half] = (core_sum(keep_ref, came_ref, 1, 0, half) + f32(low_ref[...])).astype(BF16)
    next_ref[half:] = core_sum(keep_ref, came_ref, 1, half).astype(BF16)
    last_ref[:half] = core_sum(keep_ref, came_ref, 3, 0, half).astype(BF16)
    last_ref[half:] = (core_sum(keep_ref, came_ref, 3, half) + f32(high_ref[...])).astype(BF16)


def finish_kernel(at, keep_ref, came_ref, a_ref, b_ref, residual_ref, leading_ref, summed_ref):
    total = core_sum(keep_ref, came_ref, 0) + f32(a_ref[...]) + f32(b_ref[...])
    summed_ref[...] = total
    leading_ref[...] = (f32(residual_ref[at]) + total).astype(BF16)


def end_kernel(*refs):
    out_ref = refs[-1]
    first = lax.axis_index("pipe") == 0
    at = 0
    for leading_ref, summed_ref, passed_ref in zip(refs[0:-1:3], refs[1:-1:3], refs[2:-1:3]):
        rows = leading_ref.shape[0]
        later = (f32(passed_ref[...]) + summed_ref[...]).astype(BF16)
        out_ref[0, at : at + rows, :] = jnp.where(first, leading_ref[...], later)
        at += rows


def on_device(attention_out, signs, out_weight, residual_in):
    tokens, width = attention_out.shape[1:]
    columns = out_weight.shape[2]
    scale = 1.0 / math.sqrt(width * lax.axis_size("tensor"))
    rows = tokens // 2
    cut = [slice(0, rows), slice(rows, tokens)]

    def move(value, axis, target):
        return lax.ppermute(value, axis, [(i, target(i)) for i in range(lax.axis_size(axis))])

    def ring(steps, flip=0):
        return lambda i: (i // 2 + steps) % 4 * 2 + (i % 2 ^ flip)

    def swap(value):
        return move(value, "tensor", lambda i: i ^ 1)

    def pipe(value):
        return lax.ppermute(value, "pipe", [(0, 1)])

    def pair(chunk, mine, other, behind=()):
        return call(
            "hadamard_core", lambda *refs: pair_kernel(cut[chunk], *refs), (mine, other), shape(rows, width), behind
        )

    half = rows // 2

    def up(value):
        return move(value, "tensor", ring(1))

    def down(value):
        return move(value, "tensor", ring(-1))

    def near_z(mine):
        return [mine, down(mine), up(mine)]

    def far_z(terms, behind=()):
        low, high = call("cut", cut_kernel, terms[1:], (shape(half, width),) * 2, behind)
        return terms + [up(low), down(high)]

    def mix(terms, behind=()):
        return call("hadamard_z", mix_kernel, terms, shape(rows, width), behind, weigh=20)

    def spread_column(own):
        mate = move(own, "dp", ring(0, 1))
        return [own] + [move(own, "dp", ring(-dy)) for dy in (1, 2, 3)], mate

    def spread_mate(column, mate):
        return [mate, move(mate, "dp", ring(-1)), move(column[2], "dp", ring(0, 1)), move(mate, "dp", ring(-3))]

    def far_sum(keep, came, behind=()):
        low, high = call("far_sum", far_kernel, (keep, came), (shape(half, columns),) * 2, behind)
        return up(low), down(high)

    def near_sum(keep, came, far, behind=()):
        return call("near_sum", near_kernel, (keep, came, *far), (shape(rows, columns),) * 2, behind)

    def last_sum(near):
        return up(near[0]), down(near[1])

    def finish(chunk, keep, came, arrived, behind=()):
        return call(
            "residual",
            lambda *refs: finish_kernel(cut[chunk], *refs),
            (keep, came, *arrived, residual_in),
            (shape(rows, columns), shape(rows, columns, jnp.float32)),
            behind,
            weigh=20,
        )

    local = call(
        "rotate_local",
        lambda *refs: rotate_kernel(scale, *refs),
        (attention_out, signs),
        shape(tokens, width),
        flops=2 * tokens * width * LANES,
    )
    other = swap(local)
    terms0 = near_z(pair(0, local, other))
    ready = call("weight", touch_kernel, (out_weight,), shape(8, LANES), [terms0[0]], weigh=9)
    terms0 = far_z(terms0, [ready])
    terms1 = near_z(pair(1, local, other, [terms0[1]]))
    own0 = mix(terms0, [terms1[0]])
    column0, mate0 = spread_column(own0)
    mates0 = spread_mate(column0, mate0)
    own1 = mix(far_z(terms1), mates0[1:])
    column1, mate1 = spread_column(own1)
    products0 = project(column0, out_weight, None, [own1])
    keep0, send0 = project(mates0, out_weight, products0, [mate1, *column1[1:]])
    came0 = swap(send0)
    mates1 = spread_mate(column1, mate1)
    far0 = far_sum(keep0, came0)
    products1 = project(column1, out_weight, None, [far0[0]])
    near0 = near_sum(keep0, came0, far0)
    keep1, send1 = project(mates1, out_weight, products1, [near0[0]])
    came1 = swap(send1)
    far1 = far_sum(keep1, came1)
    leading0, summed0 = finish(0, keep0, came0, last_sum(near0), [far1[0]])
    passed0 = pipe(leading0)
    near1 = near_sum(keep1, came1, far1)
    leading1, summed1 = finish(1, keep1, came1, last_sum(near1), [leading0])
    passed1 = pipe(leading1)
    return call(
        "end",
        end_kernel,
        (leading0, summed0, passed0, leading1, summed1, passed1),
        jax.ShapeDtypeStruct((1, tokens, columns), BF16),
    )


def solution(mesh):
    in_specs = (
        P("pipe", "dp", "tensor"),
        P("pipe", "tensor"),
        P("pipe", "tensor", "dp"),
        P("tensor", "dp"),
    )
    out_specs = P("pipe", "tensor", "dp")
    return jax.shard_map(
        on_device, mesh=mesh, in_specs=in_specs, out_specs=out_specs, check_vma=False
    )
```

```python
import math

import jax
import jax.numpy as jnp
from jax import lax
from jax.experimental import pallas as pl
from jax.experimental.pallas import tpu as pltpu
from jax.sharding import PartitionSpec as P

LANES = 128
BF16 = jnp.bfloat16
TILES = 4


def f32(value):
    return value.astype(jnp.float32)


def place():
    d, t = lax.axis_index("dp"), lax.axis_index("tensor")
    return d >> 1, d & 1, t >> 1, t & 1


def shape(rows, columns, kind=BF16):
    return jax.ShapeDtypeStruct((rows, columns), kind)


VMEM = pl.BlockSpec(memory_space=pltpu.VMEM)
HBM = pl.BlockSpec(memory_space=pltpu.HBM)
ANY = pl.BlockSpec(memory_space=pl.ANY)


def call(name, kernel, operands, out_shape, behind=(), specs=None, scratch=(), flops=0, limit=16, weigh=1):
    specs = specs or [VMEM] * len(operands)
    count = len(operands)
    outs = out_shape if isinstance(out_shape, tuple) else (out_shape,)
    size = sum(2 * math.prod(o.shape) for o in tuple(operands) + outs)
    return pl.pallas_call(
        lambda *refs: kernel(*refs[:count], *refs[count + len(behind) :]),
        out_shape=out_shape,
        in_specs=list(specs) + [ANY] * len(behind),
        out_specs=jax.tree.map(lambda _: VMEM, out_shape),
        scratch_shapes=list(scratch),
        compiler_params=pltpu.CompilerParams(vmem_limit_bytes=limit << 20),
        cost_estimate=pl.CostEstimate(flops=flops * weigh, bytes_accessed=size * weigh, transcendentals=0),
        name=name,
    )(*operands, *behind)


def rotate_kernel(scale, x_ref, s_ref, o_ref):
    rows, width = o_ref.shape
    pieces = width // LANES
    signs = f32(s_ref[...])
    i = lax.broadcasted_iota(jnp.int32, (LANES, LANES), 0) & lax.broadcasted_iota(jnp.int32, (LANES, LANES), 1)
    for bits in (4, 2, 1):
        i = i ^ (i >> bits)
    table = f32(1 - 2 * (i & 1)).astype(BF16)
    for r in range(0, rows, 32):
        part = []
        for a in range(pieces):
            cols = slice(a * LANES, (a + 1) * LANES)
            x = (f32(x_ref[0, r : r + 32, cols]) * signs[:, cols]).astype(BF16)
            part.append(jnp.dot(x, table, preferred_element_type=jnp.float32))
        step = 1
        while step < pieces:
            nxt = list(part)
            for a in range(pieces):
                if not a & step:
                    nxt[a] = part[a] + part[a | step]
                    nxt[a | step] = part[a] - part[a | step]
            part = nxt
            step *= 2
        for a in range(pieces):
            o_ref[r : r + 32, a * LANES : (a + 1) * LANES] = (part[a] * scale).astype(BF16)


def pair_kernel(at, mine_ref, other_ref, out_ref):
    sign = f32(1 - 2 * place()[3])
    out_ref[...] = (f32(other_ref[at]) + sign * f32(mine_ref[at])).astype(BF16)


def cut_kernel(next_ref, last_ref, low_ref, high_ref):
    half = low_ref.shape[0]
    low_ref[...] = last_ref[:half]
    high_ref[...] = next_ref[half:]


def mix_kernel(mine_ref, next_ref, last_ref, low_ref, high_ref, out_ref):
    z = place()[2]
    half = low_ref.shape[0]

    def sign(k):
        u = z & ((z + k) & 3)
        return f32(1 - 2 * ((u ^ (u >> 1)) & 1))

    for at, far_ref in ((slice(0, half), low_ref), (slice(half, 2 * half), high_ref)):
        total = sign(0) * f32(mine_ref[at]) + sign(1) * f32(next_ref[at]) + sign(3) * f32(last_ref[at])
        out_ref[at] = (total + sign(2) * f32(far_ref[...])).astype(BF16)


def touch_kernel(w_ref, out_ref):
    out_ref[...] = jnp.zeros_like(out_ref)


def products(blocks, w_ref, lhs, store):
    width = w_ref.shape[2] // TILES
    y, _, z, _ = place()
    rows = blocks[0].shape[0]
    for dy, ref in enumerate(blocks):
        lhs[pl.ds(pl.multiple_of(((y + dy - z) & 3) * rows, rows), rows), :] = ref[...]
    for n in range(TILES):
        cols = slice(n * width, (n + 1) * width)
        out = jnp.dot(lhs[...], w_ref[0, :, cols], preferred_element_type=jnp.float32)
        store(cols, out.astype(BF16))


def column_kernel(*refs):
    blocks, (w_ref, out_ref, lhs) = refs[:4], refs[4:]

    def store(cols, out):
        out_ref[:, cols] = out

    products(blocks, w_ref, lhs, store)


def mate_kernel(*refs):
    blocks, (w_ref, column_ref, keep_ref, send_ref, lhs) = refs[:4], refs[4:]
    _, x, _, c = place()

    def store(cols, out):
        @pl.when(x == c)
        def _():
            keep_ref[:, cols] = column_ref[:, cols]
            send_ref[:, cols] = out

        @pl.when(x != c)
        def _():
            keep_ref[:, cols] = out
            send_ref[:, cols] = column_ref[:, cols]

    products(blocks, w_ref, lhs, store)


def project(blocks, weight, column=None, behind=()):
    rows, depth = blocks[0].shape
    width = weight.shape[2]
    half = shape(4 * rows, width)
    return call(
        "project_column" if column is None else "project_mate",
        column_kernel if column is None else mate_kernel,
        (*blocks, weight) + (() if column is None else (column,)),
        half if column is None else (half, half),
        behind,
        scratch=[pltpu.VMEM((4 * rows, depth), BF16)],
        flops=2 * 4 * rows * depth * width,
        weigh=5,
        limit=24,
    )


def core_sum(keep_ref, came_ref, k, low=0, high=None):
    rows = keep_ref.shape[0] // 4
    at = slice(k * rows + low, k * rows + (high or rows))
    return f32(keep_ref[at]) + f32(came_ref[at])


def far_kernel(keep_ref, came_ref, low_ref, high_ref):
    half = low_ref.shape[0]
    low_ref[...] = core_sum(keep_ref, came_ref, 2, 0, half).astype(BF16)
    high_ref[...] = core_sum(keep_ref, came_ref, 2, half).astype(BF16)


def near_kernel(keep_ref, came_ref, low_ref, high_ref, next_ref, last_ref):
    half = low_ref.shape[0]
    next_ref[:half] = (core_sum(keep_ref, came_ref, 1, 0, half) + f32(low_ref[...])).astype(BF16)
    next_ref[half:] = core_sum(keep_ref, came_ref, 1, half).astype(BF16)
    last_ref[:half] = core_sum(keep_ref, came_ref, 3, 0, half).astype(BF16)
    last_ref[half:] = (core_sum(keep_ref, came_ref, 3, half) + f32(high_ref[...])).astype(BF16)


def finish_kernel(at, keep_ref, came_ref, a_ref, b_ref, residual_ref, leading_ref, summed_ref):
    total = core_sum(keep_ref, came_ref, 0) + f32(a_ref[...]) + f32(b_ref[...])
    summed_ref[...] = total
    leading_ref[...] = (f32(residual_ref[at]) + total).astype(BF16)


def end_kernel(*refs):
    out_ref = refs[-1]
    first = lax.axis_index("pipe") == 0
    at = 0
    for leading_ref, summed_ref, passed_ref in zip(refs[0:-1:3], refs[1:-1:3], refs[2:-1:3]):
        rows = leading_ref.shape[0]
        later = (f32(passed_ref[...]) + summed_ref[...]).astype(BF16)
        out_ref[0, at : at + rows, :] = jnp.where(first, leading_ref[...], later)
        at += rows


def on_device(attention_out, signs, out_weight, residual_in):
    tokens, width = attention_out.shape[1:]
    columns = out_weight.shape[2]
    scale = 1.0 / math.sqrt(width * lax.axis_size("tensor"))
    rows = tokens // 2
    cut = [slice(0, rows), slice(rows, tokens)]

    def move(value, axis, target):
        return lax.ppermute(value, axis, [(i, target(i)) for i in range(lax.axis_size(axis))])

    def ring(steps, flip=0):
        return lambda i: (i // 2 + steps) % 4 * 2 + (i % 2 ^ flip)

    def swap(value):
        return move(value, "tensor", lambda i: i ^ 1)

    def pipe(value):
        return lax.ppermute(value, "pipe", [(0, 1)])

    def pair(chunk, mine, other, behind=()):
        return call(
            "hadamard_core", lambda *refs: pair_kernel(cut[chunk], *refs), (mine, other), shape(rows, width), behind
        )

    half = rows // 2

    def up(value):
        return move(value, "tensor", ring(1))

    def down(value):
        return move(value, "tensor", ring(-1))

    def near_z(mine):
        return [mine, down(mine), up(mine)]

    def far_z(terms, behind=()):
        low, high = call("cut", cut_kernel, terms[1:], (shape(half, width),) * 2, behind)
        return terms + [up(low), down(high)]

    def mix(terms, behind=()):
        return call("hadamard_z", mix_kernel, terms, shape(rows, width), behind, weigh=20)

    def spread_column(own):
        mate = move(own, "dp", ring(0, 1))
        return [own] + [move(own, "dp", ring(-dy)) for dy in (1, 2, 3)], mate

    def hold(value, behind):
        return pl.pallas_call(
            lambda *refs: None,
            out_shape=shape(*value.shape),
            in_specs=[ANY] * (1 + len(behind)),
            out_specs=ANY,
            input_output_aliases={0: 0},
            compiler_params=pltpu.CompilerParams(vmem_limit_bytes=1 << 20),
            name="hold",
        )(value, *behind)

    def spread_mate(column, mate):
        return [mate, move(mate, "dp", ring(-1)), move(column[2], "dp", ring(0, 1)), move(mate, "dp", ring(-3))]

    def far_sum(keep, came, behind=()):
        low, high = call("far_sum", far_kernel, (keep, came), (shape(half, columns),) * 2, behind)
        return low, (up(low), down(high))

    def near_sum(keep, came, far, behind=()):
        return call("near_sum", near_kernel, (keep, came, *far), (shape(rows, columns),) * 2, behind)

    def last_sum(near):
        return up(near[0]), down(near[1])

    def finish(chunk, keep, came, arrived, behind=()):
        return call(
            "residual",
            lambda *refs: finish_kernel(cut[chunk], *refs),
            (keep, came, *arrived, residual_in),
            (shape(rows, columns), shape(rows, columns, jnp.float32)),
            behind,
            weigh=20,
        )

    local = call(
        "rotate_local",
        lambda *refs: rotate_kernel(scale, *refs),
        (attention_out, signs),
        shape(tokens, width),
        flops=2 * tokens * width * LANES,
    )
    other = swap(local)
    terms0 = near_z(pair(0, local, other))
    ready = call("weight", touch_kernel, (out_weight,), shape(8, LANES), [terms0[0]], weigh=9)
    terms0 = far_z(terms0, [ready])
    terms1 = near_z(pair(1, local, other, [terms0[1]]))
    own0 = mix(terms0, [terms1[0]])
    column0, mate0 = spread_column(own0)
    mate0 = hold(mate0, [column0[1], column0[3]])
    mates0 = spread_mate(column0, mate0)
    own1 = mix(far_z(terms1), [mates0[1], mates0[3]])
    column1, mate1 = spread_column(own1)
    products0 = project(column0, out_weight, None, [own1])
    keep0, send0 = project(mates0, out_weight, products0)
    mate1 = hold(mate1, [*column1[1:], keep0])
    came0 = swap(hold(send0, [mate1]))
    mates1 = spread_mate(column1, mate1)
    made0, far0 = far_sum(keep0, came0)
    products1 = project(column1, out_weight, None, [made0])
    near0 = near_sum(keep0, came0, far0)
    keep1, send1 = project(mates1, out_weight, products1, [near0[0]])
    came1 = swap(send1)
    made1, far1 = far_sum(keep1, came1)
    leading0, summed0 = finish(0, keep0, came0, last_sum(near0), [made1])
    passed0 = pipe(leading0)
    near1 = near_sum(keep1, came1, far1)
    leading1, summed1 = finish(1, keep1, came1, last_sum(near1), [leading0])
    passed1 = pipe(leading1)
    return call(
        "end",
        end_kernel,
        (leading0, summed0, passed0, leading1, summed1, passed1),
        jax.ShapeDtypeStruct((1, tokens, columns), BF16),
    )


def solution(mesh):
    in_specs = (
        P("pipe", "dp", "tensor"),
        P("pipe", "tensor"),
        P("pipe", "tensor", "dp"),
        P("tensor", "dp"),
    )
    out_specs = P("pipe", "tensor", "dp")
    return jax.shard_map(
        on_device, mesh=mesh, in_specs=in_specs, out_specs=out_specs, check_vma=False
    )
```

```python
import math

import jax
import jax.numpy as jnp
from jax import lax
from jax.experimental import pallas as pl
from jax.experimental.pallas import tpu as pltpu
from jax.sharding import PartitionSpec as P

LANES = 128
BF16 = jnp.bfloat16
TILES = 4
ROWS = (64, 64)
FAR = 2
STRIP = 32


def f32(value):
    return value.astype(jnp.float32)


def place():
    d, t = lax.axis_index("dp"), lax.axis_index("tensor")
    return d >> 1, d & 1, t >> 1, t & 1


def shape(rows, columns, kind=BF16):
    return jax.ShapeDtypeStruct((rows, columns), kind)


VMEM = pl.BlockSpec(memory_space=pltpu.VMEM)
HBM = pl.BlockSpec(memory_space=pltpu.HBM)
ANY = pl.BlockSpec(memory_space=pl.ANY)


def call(name, kernel, operands, out_shape, behind=(), specs=None, scratch=(), flops=0, limit=16, weigh=1):
    specs = specs or [VMEM] * len(operands)
    count = len(operands)
    outs = out_shape if isinstance(out_shape, tuple) else (out_shape,)
    size = sum(2 * math.prod(o.shape) for o in tuple(operands) + outs)
    return pl.pallas_call(
        lambda *refs: kernel(*refs[:count], *refs[count + len(behind) :]),
        out_shape=out_shape,
        in_specs=list(specs) + [ANY] * len(behind),
        out_specs=jax.tree.map(lambda _: VMEM, out_shape),
        scratch_shapes=list(scratch),
        compiler_params=pltpu.CompilerParams(vmem_limit_bytes=limit << 20),
        cost_estimate=pl.CostEstimate(flops=flops * weigh, bytes_accessed=size * weigh, transcendentals=0),
        name=name,
    )(*operands, *behind)


def rotate_kernel(scale, x_ref, s_ref, *out_refs):
    rows, width = x_ref.shape[1:]
    out_of = [(ref, r) for ref in out_refs for r in range(0, ref.shape[0], STRIP)]
    pieces = width // LANES
    signs = f32(s_ref[...])
    i = lax.broadcasted_iota(jnp.int32, (LANES, LANES), 0) & lax.broadcasted_iota(jnp.int32, (LANES, LANES), 1)
    for bits in (4, 2, 1):
        i = i ^ (i >> bits)
    table = f32(1 - 2 * (i & 1)).astype(BF16)
    for r in range(0, rows, STRIP):
        o_ref, low = out_of[r // STRIP]
        part = []
        for a in range(pieces):
            cols = slice(a * LANES, (a + 1) * LANES)
            x = (f32(x_ref[0, r : r + STRIP, cols]) * signs[:, cols]).astype(BF16)
            part.append(jnp.dot(x, table, preferred_element_type=jnp.float32))
        step = 1
        while step < pieces:
            nxt = list(part)
            for a in range(pieces):
                if not a & step:
                    nxt[a] = part[a] + part[a | step]
                    nxt[a | step] = part[a] - part[a | step]
            part = nxt
            step *= 2
        for a in range(pieces):
            o_ref[low : low + STRIP, a * LANES : (a + 1) * LANES] = (part[a] * scale).astype(BF16)


def pair_kernel(mine_ref, other_ref, out_ref):
    sign = f32(1 - 2 * place()[3])
    out_ref[...] = (f32(other_ref[...]) + sign * f32(mine_ref[...])).astype(BF16)


def cut_kernel(next_ref, last_ref, low_ref, high_ref):
    half = low_ref.shape[1]
    low_ref[...] = last_ref[:, :half]
    high_ref[...] = next_ref[:, half:]


def mix_kernel(mine_ref, next_ref, last_ref, low_ref, high_ref, out_ref):
    z = place()[2]
    half = low_ref.shape[1]

    def sign(k):
        u = z & ((z + k) & 3)
        return f32(1 - 2 * ((u ^ (u >> 1)) & 1))

    for at, far_ref in ((slice(0, half), low_ref), (slice(half, 2 * half), high_ref)):
        total = sign(0) * f32(mine_ref[:, at]) + sign(1) * f32(next_ref[:, at]) + sign(3) * f32(last_ref[:, at])
        out_ref[:, at] = (total + sign(2) * f32(far_ref[...])).astype(BF16)


def touch_kernel(w_ref, out_ref):
    out_ref[...] = jnp.zeros_like(out_ref)


def products(blocks, w_ref, lhs, store):
    width = w_ref.shape[2] // TILES
    y, _, z, _ = place()
    rows = blocks[0].shape[0]
    for dy, ref in enumerate(blocks):
        lhs[pl.ds(pl.multiple_of(((y + dy - z) & 3) * rows, rows), rows), :] = ref[...]
    for n in range(TILES):
        cols = slice(n * width, (n + 1) * width)
        out = jnp.dot(lhs[...], w_ref[0, :, cols], preferred_element_type=jnp.float32)
        store(cols, out.astype(BF16))


def column_kernel(*refs):
    blocks, (w_ref, out_ref, lhs) = refs[:4], refs[4:]

    def store(cols, out):
        out_ref[:, cols] = out

    products(blocks, w_ref, lhs, store)


def mate_kernel(*refs):
    blocks, (w_ref, column_ref, keep_ref, far_ref, near_ref, lhs) = refs[:4], refs[4:]
    _, x, _, c = place()
    rows = far_ref.shape[0]

    def send(cols, value):
        far_ref[:, cols] = value[FAR * rows : (FAR + 1) * rows]
        near_ref[: FAR * rows, cols] = value[: FAR * rows]
        near_ref[FAR * rows :, cols] = value[(FAR + 1) * rows :]

    def store(cols, out):
        @pl.when(x == c)
        def _():
            keep_ref[:, cols] = column_ref[:, cols]
            send(cols, out)

        @pl.when(x != c)
        def _():
            keep_ref[:, cols] = out
            send(cols, column_ref[:, cols])

    products(blocks, w_ref, lhs, store)


def project(blocks, weight, column=None, behind=()):
    rows, depth = blocks[0].shape
    width = weight.shape[2]
    half = shape(4 * rows, width)
    return call(
        "project_column" if column is None else "project_mate",
        column_kernel if column is None else mate_kernel,
        (*blocks, weight) + (() if column is None else (column,)),
        half if column is None else (half, shape(rows, width), shape(3 * rows, width)),
        behind,
        scratch=[pltpu.VMEM((4 * rows, depth), BF16)],
        flops=2 * 4 * rows * depth * width,
        weigh=5,
        limit=24,
    )


def core_sum(keep_ref, came_ref, k, cols=slice(None)):
    rows = keep_ref.shape[0] // 4
    place = k - (k > FAR)
    came = came_ref[...] if k == FAR else came_ref[place * rows : (place + 1) * rows]
    return (f32(keep_ref[k * rows : (k + 1) * rows]) + f32(came))[:, cols]


def far_kernel(keep_ref, came_ref, low_ref, high_ref):
    half = low_ref.shape[1]
    low_ref[...] = core_sum(keep_ref, came_ref, FAR, slice(0, half)).astype(BF16)
    high_ref[...] = core_sum(keep_ref, came_ref, FAR, slice(half, None)).astype(BF16)


def near_kernel(keep_ref, came_ref, low_ref, high_ref, next_ref, last_ref):
    half = low_ref.shape[1]
    low, high = slice(0, half), slice(half, None)
    next_ref[:, low] = (core_sum(keep_ref, came_ref, 1, low) + f32(low_ref[...])).astype(BF16)
    next_ref[:, high] = core_sum(keep_ref, came_ref, 1, high).astype(BF16)
    last_ref[:, low] = core_sum(keep_ref, came_ref, 3, low).astype(BF16)
    last_ref[:, high] = (core_sum(keep_ref, came_ref, 3, high) + f32(high_ref[...])).astype(BF16)


def finish_kernel(at, keep_ref, came_ref, a_ref, b_ref, residual_ref, leading_ref, summed_ref):
    total = core_sum(keep_ref, came_ref, 0) + f32(a_ref[...]) + f32(b_ref[...])
    summed_ref[...] = total
    leading_ref[...] = (f32(residual_ref[at]) + total).astype(BF16)


def end_kernel(*refs):
    out_ref = refs[-1]
    first = lax.axis_index("pipe") == 0
    at = 0
    for leading_ref, summed_ref, passed_ref in zip(refs[0:-1:3], refs[1:-1:3], refs[2:-1:3]):
        rows = leading_ref.shape[0]
        later = (f32(passed_ref[...]) + summed_ref[...]).astype(BF16)
        out_ref[0, at : at + rows, :] = jnp.where(first, leading_ref[...], later)
        at += rows


def on_device(attention_out, signs, out_weight, residual_in):
    tokens, width = attention_out.shape[1:]
    columns = out_weight.shape[2]
    scale = 1.0 / math.sqrt(width * lax.axis_size("tensor"))
    cut = [slice(0, ROWS[0]), slice(ROWS[0], tokens)]

    def move(value, axis, target):
        return lax.ppermute(value, axis, [(i, target(i)) for i in range(lax.axis_size(axis))])

    def ring(steps, flip=0):
        return lambda i: (i // 2 + steps) % 4 * 2 + (i % 2 ^ flip)

    def swap(value):
        return move(value, "tensor", lambda i: i ^ 1)

    def pipe(value):
        return lax.ppermute(value, "pipe", [(0, 1)])

    def pair(mine, other, behind=()):
        return call("hadamard_core", pair_kernel, (mine, other), shape(*mine.shape), behind)

    def up(value):
        return move(value, "tensor", ring(1))

    def down(value):
        return move(value, "tensor", ring(-1))

    def near_z(mine):
        return [mine, down(mine), up(mine)]

    def far_z(terms, behind=()):
        low, high = call("cut", cut_kernel, terms[1:], (shape(terms[0].shape[0], width // 2),) * 2, behind)
        return terms + [up(low), down(high)]

    def mix(terms, behind=()):
        return call("hadamard_z", mix_kernel, terms, shape(*terms[0].shape), behind, weigh=20)

    def spread_column(own):
        mate = move(own, "dp", ring(0, 1))
        return [own] + [move(own, "dp", ring(-dy)) for dy in (1, 2, 3)], mate

    def hold(value, behind):
        return pl.pallas_call(
            lambda *refs: None,
            out_shape=shape(*value.shape),
            in_specs=[ANY] * (1 + len(behind)),
            out_specs=ANY,
            input_output_aliases={0: 0},
            compiler_params=pltpu.CompilerParams(vmem_limit_bytes=1 << 20),
            name="hold",
        )(value, *behind)

    def spread_mate(column, mate):
        return [mate, move(mate, "dp", ring(-1)), move(column[2], "dp", ring(0, 1)), move(mate, "dp", ring(-3))]

    def far_sum(keep, came, behind=()):
        low, high = call("far_sum", far_kernel, (keep, came), (shape(came.shape[0], columns // 2),) * 2, behind)
        return low, (up(low), down(high))

    def near_sum(keep, came, far, behind=()):
        return call("near_sum", near_kernel, (keep, came, *far), (shape(far[0].shape[0], columns),) * 2, behind)

    def last_sum(near):
        return up(near[0]), down(near[1])

    def finish(chunk, keep, came, arrived, behind=()):
        return call(
            "residual",
            lambda *refs: finish_kernel(cut[chunk], *refs),
            (keep, came, *arrived, residual_in),
            (shape(ROWS[chunk], columns), shape(ROWS[chunk], columns, jnp.float32)),
            behind,
            weigh=20,
        )

    local = call(
        "rotate_local",
        lambda *refs: rotate_kernel(scale, *refs),
        (attention_out, signs),
        tuple(shape(rows, width) for rows in ROWS),
        flops=2 * tokens * width * LANES,
    )
    other = [swap(local[0]), swap(local[1])]
    terms0 = near_z(pair(local[0], other[0]))
    ready = call("weight", touch_kernel, (out_weight,), shape(8, LANES), [terms0[0]], weigh=9)
    terms0 = far_z(terms0, [ready])
    terms1 = near_z(pair(local[1], other[1], [terms0[1]]))
    own0 = mix(terms0, [terms1[0]])
    column0, mate0 = spread_column(own0)
    mate0 = hold(mate0, [column0[1], column0[3]])
    mates0 = spread_mate(column0, mate0)
    own1 = mix(far_z(terms1), [mates0[1], mates0[3]])
    column1, mate1 = spread_column(own1)
    products0 = project(column0, out_weight, None, [own1])
    keep0, far0, near0 = project(mates0, out_weight, products0)
    mate1 = hold(mate1, [*column1[1:], keep0])
    far0 = swap(hold(far0, [mate1]))
    made0, ring0 = far_sum(keep0, far0)
    near0 = swap(hold(near0, [far0]))
    mates1 = spread_mate(column1, hold(mate1, [made0, near0]))
    sums0 = near_sum(keep0, near0, ring0)
    products1 = project(column1, out_weight, None, [sums0[0]])
    keep1, far1, near1 = project(mates1, out_weight, products1)
    last0 = last_sum(sums0)
    far1 = swap(hold(far1, last0))
    near1 = swap(hold(near1, [far1]))
    made1, ring1 = far_sum(keep1, far1)
    leading0, summed0 = finish(0, keep0, near0, last0, [made1])
    passed0 = pipe(leading0)
    sums1 = near_sum(keep1, near1, ring1)
    leading1, summed1 = finish(1, keep1, near1, last_sum(sums1), [leading0])
    passed1 = pipe(leading1)
    return call(
        "end",
        end_kernel,
        (leading0, summed0, passed0, leading1, summed1, passed1),
        jax.ShapeDtypeStruct((1, tokens, columns), BF16),
    )


def solution(mesh):
    in_specs = (
        P("pipe", "dp", "tensor"),
        P("pipe", "tensor"),
        P("pipe", "tensor", "dp"),
        P("tensor", "dp"),
    )
    out_specs = P("pipe", "tensor", "dp")
    return jax.shard_map(
        on_device, mesh=mesh, in_specs=in_specs, out_specs=out_specs, check_vma=False
    )
```

```python
import math

import jax
import jax.numpy as jnp
from jax import lax
from jax.experimental import pallas as pl
from jax.experimental.pallas import tpu as pltpu
from jax.sharding import PartitionSpec as P

LANES = 128
BF16 = jnp.bfloat16
TILES = 4
ROWS = (64, 64)
PARTS = (32, 32)
FAR = 2
STRIP = 32


def f32(value):
    return value.astype(jnp.float32)


def place():
    d, t = lax.axis_index("dp"), lax.axis_index("tensor")
    return d >> 1, d & 1, t >> 1, t & 1


def shape(rows, columns, kind=BF16):
    return jax.ShapeDtypeStruct((rows, columns), kind)


VMEM = pl.BlockSpec(memory_space=pltpu.VMEM)
HBM = pl.BlockSpec(memory_space=pltpu.HBM)
ANY = pl.BlockSpec(memory_space=pl.ANY)


def call(name, kernel, operands, out_shape, behind=(), specs=None, scratch=(), flops=0, limit=16, weigh=1):
    specs = specs or [VMEM] * len(operands)
    count = len(operands)
    outs = out_shape if isinstance(out_shape, tuple) else (out_shape,)
    size = sum(2 * math.prod(o.shape) for o in tuple(operands) + outs)
    return pl.pallas_call(
        lambda *refs: kernel(*refs[:count], *refs[count + len(behind) :]),
        out_shape=out_shape,
        in_specs=list(specs) + [ANY] * len(behind),
        out_specs=jax.tree.map(lambda _: VMEM, out_shape),
        scratch_shapes=list(scratch),
        compiler_params=pltpu.CompilerParams(vmem_limit_bytes=limit << 20),
        cost_estimate=pl.CostEstimate(flops=flops * weigh, bytes_accessed=size * weigh, transcendentals=0),
        name=name,
    )(*operands, *behind)


def rotate_kernel(scale, x_ref, s_ref, *out_refs):
    rows, width = x_ref.shape[1:]
    out_of = [(ref, r) for ref in out_refs for r in range(0, ref.shape[0], STRIP)]
    pieces = width // LANES
    signs = f32(s_ref[...])
    i = lax.broadcasted_iota(jnp.int32, (LANES, LANES), 0) & lax.broadcasted_iota(jnp.int32, (LANES, LANES), 1)
    for bits in (4, 2, 1):
        i = i ^ (i >> bits)
    table = f32(1 - 2 * (i & 1)).astype(BF16)
    for r in range(0, rows, STRIP):
        o_ref, low = out_of[r // STRIP]
        part = []
        for a in range(pieces):
            cols = slice(a * LANES, (a + 1) * LANES)
            x = (f32(x_ref[0, r : r + STRIP, cols]) * signs[:, cols]).astype(BF16)
            part.append(jnp.dot(x, table, preferred_element_type=jnp.float32))
        step = 1
        while step < pieces:
            nxt = list(part)
            for a in range(pieces):
                if not a & step:
                    nxt[a] = part[a] + part[a | step]
                    nxt[a | step] = part[a] - part[a | step]
            part = nxt
            step *= 2
        for a in range(pieces):
            o_ref[low : low + STRIP, a * LANES : (a + 1) * LANES] = (part[a] * scale).astype(BF16)


def pair_kernel(mine_ref, other_ref, out_ref):
    sign = f32(1 - 2 * place()[3])
    out_ref[...] = (f32(other_ref[...]) + sign * f32(mine_ref[...])).astype(BF16)


def cut_kernel(next_ref, last_ref, low_ref, high_ref):
    half = low_ref.shape[1]
    low_ref[...] = last_ref[:, :half]
    high_ref[...] = next_ref[:, half:]


def mix_kernel(mine_ref, next_ref, last_ref, low_ref, high_ref, out_ref):
    z = place()[2]
    half = low_ref.shape[1]

    def sign(k):
        u = z & ((z + k) & 3)
        return f32(1 - 2 * ((u ^ (u >> 1)) & 1))

    for at, far_ref in ((slice(0, half), low_ref), (slice(half, 2 * half), high_ref)):
        total = sign(0) * f32(mine_ref[:, at]) + sign(1) * f32(next_ref[:, at]) + sign(3) * f32(last_ref[:, at])
        out_ref[:, at] = (total + sign(2) * f32(far_ref[...])).astype(BF16)


def touch_kernel(w_ref, out_ref):
    out_ref[...] = jnp.zeros_like(out_ref)


def products(blocks, w_ref, lhs, store):
    width = w_ref.shape[2] // TILES
    y, _, z, _ = place()
    rows = blocks[0].shape[0]
    for dy, ref in enumerate(blocks):
        lhs[pl.ds(pl.multiple_of(((y + dy - z) & 3) * rows, rows), rows), :] = ref[...]
    for n in range(TILES):
        cols = slice(n * width, (n + 1) * width)
        out = jnp.dot(lhs[...], w_ref[0, :, cols], preferred_element_type=jnp.float32)
        store(cols, out.astype(BF16))


def column_kernel(*refs):
    blocks, (w_ref, out_ref, lhs) = refs[:4], refs[4:]

    def store(cols, out):
        out_ref[:, cols] = out

    products(blocks, w_ref, lhs, store)


def mate_kernel(*refs):
    blocks, (w_ref, column_ref, keep_ref, far_ref, near_ref, lhs) = refs[:4], refs[4:]
    _, x, _, c = place()
    rows = far_ref.shape[0]

    def send(cols, value):
        far_ref[:, cols] = value[FAR * rows : (FAR + 1) * rows]
        near_ref[: FAR * rows, cols] = value[: FAR * rows]
        near_ref[FAR * rows :, cols] = value[(FAR + 1) * rows :]

    def store(cols, out):
        @pl.when(x == c)
        def _():
            keep_ref[:, cols] = column_ref[:, cols]
            send(cols, out)

        @pl.when(x != c)
        def _():
            keep_ref[:, cols] = out
            send(cols, column_ref[:, cols])

    products(blocks, w_ref, lhs, store)


def project(blocks, weight, column=None, behind=()):
    rows, depth = blocks[0].shape
    width = weight.shape[2]
    half = shape(4 * rows, width)
    return call(
        "project_column" if column is None else "project_mate",
        column_kernel if column is None else mate_kernel,
        (*blocks, weight) + (() if column is None else (column,)),
        half if column is None else (half, shape(rows, width), shape(3 * rows, width)),
        behind,
        scratch=[pltpu.VMEM((4 * rows, depth), BF16)],
        flops=2 * 4 * rows * depth * width,
        weigh=5,
        limit=24,
    )


def core_sum(keep_ref, came_ref, k, cols=slice(None)):
    rows = keep_ref.shape[0] // 4
    place = k - (k > FAR)
    came = came_ref[...] if k == FAR else came_ref[place * rows : (place + 1) * rows]
    return (f32(keep_ref[k * rows : (k + 1) * rows]) + f32(came))[:, cols]


def far_kernel(keep_ref, came_ref, low_ref, high_ref):
    half = low_ref.shape[1]
    low_ref[...] = core_sum(keep_ref, came_ref, FAR, slice(0, half)).astype(BF16)
    high_ref[...] = core_sum(keep_ref, came_ref, FAR, slice(half, None)).astype(BF16)


def near_kernel(keep_ref, came_ref, low_ref, high_ref, *out_refs):
    half = low_ref.shape[1]
    low, high = slice(0, half), slice(half, None)
    at = 0
    for next_ref, last_ref in zip(out_refs[::2], out_refs[1::2]):
        part = slice(at, at + next_ref.shape[0])
        at = part.stop
        next_ref[:, low] = (core_sum(keep_ref, came_ref, 1, low)[part] + f32(low_ref[part])).astype(BF16)
        next_ref[:, high] = core_sum(keep_ref, came_ref, 1, high)[part].astype(BF16)
        last_ref[:, low] = core_sum(keep_ref, came_ref, 3, low)[part].astype(BF16)
        last_ref[:, high] = (core_sum(keep_ref, came_ref, 3, high)[part] + f32(high_ref[part])).astype(BF16)


def finish_kernel(at, low, keep_ref, came_ref, a_ref, b_ref, residual_ref, leading_ref, summed_ref):
    rows = leading_ref.shape[0]
    total = core_sum(keep_ref, came_ref, 0)[low : low + rows] + f32(a_ref[...]) + f32(b_ref[...])
    summed_ref[...] = total
    leading_ref[...] = (f32(residual_ref[at : at + rows]) + total).astype(BF16)


def end_rows(refs, out_ref, at):
    first = lax.axis_index("pipe") == 0
    for leading_ref, summed_ref, passed_ref in zip(refs[0::3], refs[1::3], refs[2::3]):
        rows = leading_ref.shape[0]
        later = (f32(passed_ref[...]) + summed_ref[...]).astype(BF16)
        out_ref[at : at + rows, :] = jnp.where(first, leading_ref[...], later)
        at += rows


def early_kernel(*refs):
    end_rows(refs[:-1], refs[-1], 0)


def end_kernel(early_ref, *refs):
    rows = early_ref.shape[0]
    refs[-1][0, :rows] = early_ref[...]
    end_rows(refs[:-1], refs[-1].at[0], rows)


def on_device(attention_out, signs, out_weight, residual_in):
    tokens, width = attention_out.shape[1:]
    columns = out_weight.shape[2]
    scale = 1.0 / math.sqrt(width * lax.axis_size("tensor"))
    cut = [slice(0, ROWS[0]), slice(ROWS[0], tokens)]

    def move(value, axis, target):
        return lax.ppermute(value, axis, [(i, target(i)) for i in range(lax.axis_size(axis))])

    def ring(steps, flip=0):
        return lambda i: (i // 2 + steps) % 4 * 2 + (i % 2 ^ flip)

    def swap(value):
        return move(value, "tensor", lambda i: i ^ 1)

    def pipe(value):
        return lax.ppermute(value, "pipe", [(0, 1)])

    def pair(mine, other, behind=()):
        return call("hadamard_core", pair_kernel, (mine, other), shape(*mine.shape), behind)

    def up(value):
        return move(value, "tensor", ring(1))

    def down(value):
        return move(value, "tensor", ring(-1))

    def near_z(mine):
        return [mine, down(mine), up(mine)]

    def far_z(terms, behind=()):
        low, high = call("cut", cut_kernel, terms[1:], (shape(terms[0].shape[0], width // 2),) * 2, behind)
        return terms + [up(low), down(high)]

    def mix(terms, behind=()):
        return call("hadamard_z", mix_kernel, terms, shape(*terms[0].shape), behind, weigh=20)

    def spread_column(own):
        mate = move(own, "dp", ring(0, 1))
        return [own] + [move(own, "dp", ring(-dy)) for dy in (1, 2, 3)], mate

    def hold(value, behind):
        return pl.pallas_call(
            lambda *refs: None,
            out_shape=shape(*value.shape),
            in_specs=[ANY] * (1 + len(behind)),
            out_specs=ANY,
            input_output_aliases={0: 0},
            compiler_params=pltpu.CompilerParams(vmem_limit_bytes=1 << 20),
            name="hold",
        )(value, *behind)

    def spread_mate(column, mate):
        return [mate, move(mate, "dp", ring(-1)), move(column[2], "dp", ring(0, 1)), move(mate, "dp", ring(-3))]

    def far_sum(keep, came, behind=()):
        low, high = call("far_sum", far_kernel, (keep, came), (shape(came.shape[0], columns // 2),) * 2, behind)
        return low, (up(low), down(high))

    def near_sum(keep, came, far, parts, behind=()):
        outs = [shape(rows, columns) for rows in parts for _ in range(2)]
        return call("near_sum", near_kernel, (keep, came, *far), tuple(outs), behind)

    def last_sum(near):
        return up(near[0]), down(near[1])

    def finish(at, low, keep, came, arrived, behind=()):
        rows = arrived[0].shape[0]
        return call(
            "residual",
            lambda *refs: finish_kernel(at, low, *refs),
            (keep, came, *arrived, residual_in),
            (shape(rows, columns), shape(rows, columns, jnp.float32)),
            behind,
            weigh=20,
        )

    local = call(
        "rotate_local",
        lambda *refs: rotate_kernel(scale, *refs),
        (attention_out, signs),
        tuple(shape(rows, width) for rows in ROWS),
        flops=2 * tokens * width * LANES,
    )
    other = [swap(local[0]), swap(local[1])]
    terms0 = near_z(pair(local[0], other[0]))
    ready = call("weight", touch_kernel, (out_weight,), shape(8, LANES), [terms0[0]], weigh=9)
    terms0 = far_z(terms0, [ready])
    terms1 = near_z(pair(local[1], other[1], [terms0[1]]))
    own0 = mix(terms0, [terms1[0]])
    column0, mate0 = spread_column(own0)
    mate0 = hold(mate0, [column0[1], column0[3]])
    mates0 = spread_mate(column0, mate0)
    own1 = mix(far_z(terms1), [mates0[1], mates0[3]])
    column1, mate1 = spread_column(own1)
    products0 = project(column0, out_weight, None, [own1])
    keep0, far0, near0 = project(mates0, out_weight, products0)
    mate1 = hold(mate1, [*column1[1:], keep0])
    far0 = swap(hold(far0, [mate1]))
    made0, ring0 = far_sum(keep0, far0)
    near0 = swap(hold(near0, [far0]))
    mates1 = spread_mate(column1, hold(mate1, [made0, near0]))
    sums0 = near_sum(keep0, near0, ring0, ROWS[:1])
    products1 = project(column1, out_weight, None, [sums0[0]])
    keep1, far1, near1 = project(mates1, out_weight, products1)
    last0 = last_sum(sums0)
    far1 = swap(hold(far1, last0))
    near1 = swap(hold(near1, [far1]))
    made1, ring1 = far_sum(keep1, far1)
    leading0, summed0 = finish(0, 0, keep0, near0, last0, [made1])
    passed0 = pipe(leading0)
    sums1 = near_sum(keep1, near1, ring1, PARTS)
    leading1, summed1 = finish(ROWS[0], 0, keep1, near1, last_sum(sums1[:2]), [leading0, passed0])
    passed1 = pipe(leading1)
    leading2, summed2 = finish(ROWS[0] + PARTS[0], PARTS[0], keep1, near1, last_sum(sums1[2:]), [leading1])
    passed2 = pipe(leading2)
    early = call(
        "early",
        early_kernel,
        (leading0, summed0, passed0, leading1, summed1, passed1),
        shape(tokens - PARTS[1], columns),
        weigh=20,
    )
    return call(
        "end",
        end_kernel,
        (early, leading2, summed2, passed2),
        jax.ShapeDtypeStruct((1, tokens, columns), BF16),
    )


def solution(mesh):
    in_specs = (
        P("pipe", "dp", "tensor"),
        P("pipe", "tensor"),
        P("pipe", "tensor", "dp"),
        P("tensor", "dp"),
    )
    out_specs = P("pipe", "tensor", "dp")
    return jax.shard_map(
        on_device, mesh=mesh, in_specs=in_specs, out_specs=out_specs, check_vma=False
    )
```

```python
import math

import jax
import jax.numpy as jnp
from jax import lax
from jax.experimental import pallas as pl
from jax.experimental.pallas import tpu as pltpu
from jax.sharding import PartitionSpec as P

LANES = 128
BF16 = jnp.bfloat16
TILES = 4
ROWS = (64, 64)
PARTS = (32, 32)
FAR = 2
STRIP = 32


def f32(value):
    return value.astype(jnp.float32)


def place():
    d, t = lax.axis_index("dp"), lax.axis_index("tensor")
    return d >> 1, d & 1, t >> 1, t & 1


def shape(rows, columns, kind=BF16):
    return jax.ShapeDtypeStruct((rows, columns), kind)


VMEM = pl.BlockSpec(memory_space=pltpu.VMEM)
HBM = pl.BlockSpec(memory_space=pltpu.HBM)
ANY = pl.BlockSpec(memory_space=pl.ANY)


def call(name, kernel, operands, out_shape, behind=(), specs=None, scratch=(), flops=0, limit=16, weigh=1):
    specs = specs or [VMEM] * len(operands)
    count = len(operands)
    outs = out_shape if isinstance(out_shape, tuple) else (out_shape,)
    size = sum(2 * math.prod(o.shape) for o in tuple(operands) + outs)
    return pl.pallas_call(
        lambda *refs: kernel(*refs[:count], *refs[count + len(behind) :]),
        out_shape=out_shape,
        in_specs=list(specs) + [ANY] * len(behind),
        out_specs=jax.tree.map(lambda _: VMEM, out_shape),
        scratch_shapes=list(scratch),
        compiler_params=pltpu.CompilerParams(vmem_limit_bytes=limit << 20),
        cost_estimate=pl.CostEstimate(flops=flops * weigh, bytes_accessed=size * weigh, transcendentals=0),
        name=name,
    )(*operands, *behind)


def rotate_kernel(scale, x_ref, s_ref, *out_refs):
    rows, width = x_ref.shape[1:]
    out_of = [(ref, r) for ref in out_refs for r in range(0, ref.shape[0], STRIP)]
    pieces = width // LANES
    signs = f32(s_ref[...])
    i = lax.broadcasted_iota(jnp.int32, (LANES, LANES), 0) & lax.broadcasted_iota(jnp.int32, (LANES, LANES), 1)
    for bits in (4, 2, 1):
        i = i ^ (i >> bits)
    table = f32(1 - 2 * (i & 1)).astype(BF16)
    for r in range(0, rows, STRIP):
        o_ref, low = out_of[r // STRIP]
        part = []
        for a in range(pieces):
            cols = slice(a * LANES, (a + 1) * LANES)
            x = (f32(x_ref[0, r : r + STRIP, cols]) * signs[:, cols]).astype(BF16)
            part.append(jnp.dot(x, table, preferred_element_type=jnp.float32))
        step = 1
        while step < pieces:
            nxt = list(part)
            for a in range(pieces):
                if not a & step:
                    nxt[a] = part[a] + part[a | step]
                    nxt[a | step] = part[a] - part[a | step]
            part = nxt
            step *= 2
        for a in range(pieces):
            o_ref[low : low + STRIP, a * LANES : (a + 1) * LANES] = (part[a] * scale).astype(BF16)


def pair_kernel(mine_ref, other_ref, out_ref):
    sign = f32(1 - 2 * place()[3])
    out_ref[...] = (f32(other_ref[...]) + sign * f32(mine_ref[...])).astype(BF16)


def cut_kernel(next_ref, last_ref, low_ref, high_ref):
    half = low_ref.shape[1]
    low_ref[...] = last_ref[:, :half]
    high_ref[...] = next_ref[:, half:]


def mix_kernel(mine_ref, next_ref, last_ref, low_ref, high_ref, out_ref):
    z = place()[2]
    half = low_ref.shape[1]

    def sign(k):
        u = z & ((z + k) & 3)
        return f32(1 - 2 * ((u ^ (u >> 1)) & 1))

    for at, far_ref in ((slice(0, half), low_ref), (slice(half, 2 * half), high_ref)):
        total = sign(0) * f32(mine_ref[:, at]) + sign(1) * f32(next_ref[:, at]) + sign(3) * f32(last_ref[:, at])
        out_ref[:, at] = (total + sign(2) * f32(far_ref[...])).astype(BF16)


def touch_kernel(w_ref, out_ref):
    out_ref[...] = jnp.zeros_like(out_ref)


def products(blocks, w_ref, lhs, store):
    width = w_ref.shape[2] // TILES
    y, _, z, _ = place()
    rows = blocks[0].shape[0]
    for dy, ref in enumerate(blocks):
        lhs[pl.ds(pl.multiple_of(((y + dy - z) & 3) * rows, rows), rows), :] = ref[...]
    for n in range(TILES):
        cols = slice(n * width, (n + 1) * width)
        out = jnp.dot(lhs[...], w_ref[0, :, cols], preferred_element_type=jnp.float32)
        store(cols, out.astype(BF16))


def column_kernel(*refs):
    blocks, (w_ref, out_ref, lhs) = refs[:4], refs[4:]

    def store(cols, out):
        out_ref[:, cols] = out

    products(blocks, w_ref, lhs, store)


def mate_kernel(*refs):
    blocks, (w_ref, column_ref, keep_ref, far_ref, near_ref, lhs) = refs[:4], refs[4:]
    _, x, _, c = place()
    rows = far_ref.shape[0]

    def send(cols, value):
        far_ref[:, cols] = value[FAR * rows : (FAR + 1) * rows]
        near_ref[: FAR * rows, cols] = value[: FAR * rows]
        near_ref[FAR * rows :, cols] = value[(FAR + 1) * rows :]

    def store(cols, out):
        @pl.when(x == c)
        def _():
            keep_ref[:, cols] = column_ref[:, cols]
            send(cols, out)

        @pl.when(x != c)
        def _():
            keep_ref[:, cols] = out
            send(cols, column_ref[:, cols])

    products(blocks, w_ref, lhs, store)


def project(blocks, weight, column=None, behind=()):
    rows, depth = blocks[0].shape
    width = weight.shape[2]
    half = shape(4 * rows, width)
    return call(
        "project_column" if column is None else "project_mate",
        column_kernel if column is None else mate_kernel,
        (*blocks, weight) + (() if column is None else (column,)),
        half if column is None else (half, shape(rows, width), shape(3 * rows, width)),
        behind,
        scratch=[pltpu.VMEM((4 * rows, depth), BF16)],
        flops=2 * 4 * rows * depth * width,
        weigh=5,
        limit=24,
    )


def core_sum(keep_ref, came_ref, k, cols=slice(None)):
    rows = keep_ref.shape[0] // 4
    place = k - (k > FAR)
    came = came_ref[...] if k == FAR else came_ref[place * rows : (place + 1) * rows]
    return (f32(keep_ref[k * rows : (k + 1) * rows]) + f32(came))[:, cols]


def far_kernel(keep_ref, came_ref, low_ref, high_ref):
    half = low_ref.shape[1]
    low_ref[...] = core_sum(keep_ref, came_ref, FAR, slice(0, half)).astype(BF16)
    high_ref[...] = core_sum(keep_ref, came_ref, FAR, slice(half, None)).astype(BF16)


def near_kernel(keep_ref, came_ref, low_ref, high_ref, *out_refs):
    half = low_ref.shape[1]
    low, high = slice(0, half), slice(half, None)
    at = 0
    for next_ref, last_ref in zip(out_refs[::2], out_refs[1::2]):
        part = slice(at, at + next_ref.shape[0])
        at = part.stop
        next_ref[:, low] = (core_sum(keep_ref, came_ref, 1, low)[part] + f32(low_ref[part])).astype(BF16)
        next_ref[:, high] = core_sum(keep_ref, came_ref, 1, high)[part].astype(BF16)
        last_ref[:, low] = core_sum(keep_ref, came_ref, 3, low)[part].astype(BF16)
        last_ref[:, high] = (core_sum(keep_ref, came_ref, 3, high)[part] + f32(high_ref[part])).astype(BF16)


def finish_kernel(at, low, keep_ref, came_ref, a_ref, b_ref, residual_ref, leading_ref, summed_ref):
    rows = leading_ref.shape[0]
    total = core_sum(keep_ref, came_ref, 0)[low : low + rows] + f32(a_ref[...]) + f32(b_ref[...])
    summed_ref[...] = total
    leading_ref[...] = (f32(residual_ref[at : at + rows]) + total).astype(BF16)


def end_rows(refs, out_ref, at):
    first = lax.axis_index("pipe") == 0
    for leading_ref, summed_ref, passed_ref in zip(refs[0::3], refs[1::3], refs[2::3]):
        rows = leading_ref.shape[0]
        later = (f32(passed_ref[...]) + summed_ref[...]).astype(BF16)
        out_ref[at : at + rows, :] = jnp.where(first, leading_ref[...], later)
        at += rows


def early_kernel(*refs):
    end_rows(refs[:-1], refs[-1], 0)


def end_kernel(early_ref, *refs):
    rows = early_ref.shape[0]
    refs[-1][0, :rows] = early_ref[...]
    end_rows(refs[:-1], refs[-1].at[0], rows)


def on_device(attention_out, signs, out_weight, residual_in):
    tokens, width = attention_out.shape[1:]
    columns = out_weight.shape[2]
    scale = 1.0 / math.sqrt(width * lax.axis_size("tensor"))
    cut = [slice(0, ROWS[0]), slice(ROWS[0], tokens)]

    def move(value, axis, target):
        return lax.ppermute(value, axis, [(i, target(i)) for i in range(lax.axis_size(axis))])

    def ring(steps, flip=0):
        return lambda i: (i // 2 + steps) % 4 * 2 + (i % 2 ^ flip)

    def swap(value):
        return move(value, "tensor", lambda i: i ^ 1)

    def pipe(value):
        return lax.ppermute(value, "pipe", [(0, 1), (1, 0)])

    def pair(mine, other, behind=()):
        return call("hadamard_core", pair_kernel, (mine, other), shape(*mine.shape), behind)

    def up(value):
        return move(value, "tensor", ring(1))

    def down(value):
        return move(value, "tensor", ring(-1))

    def near_z(mine):
        return [mine, down(mine), up(mine)]

    def far_z(terms, behind=()):
        low, high = call("cut", cut_kernel, terms[1:], (shape(terms[0].shape[0], width // 2),) * 2, behind)
        return terms + [up(low), down(high)]

    def mix(terms, behind=()):
        return call("hadamard_z", mix_kernel, terms, shape(*terms[0].shape), behind, weigh=20)

    def spread_column(own):
        mate = move(own, "dp", ring(0, 1))
        return [own] + [move(own, "dp", ring(-dy)) for dy in (1, 2, 3)], mate

    def hold(value, behind):
        return pl.pallas_call(
            lambda *refs: None,
            out_shape=shape(*value.shape),
            in_specs=[ANY] * (1 + len(behind)),
            out_specs=ANY,
            input_output_aliases={0: 0},
            compiler_params=pltpu.CompilerParams(vmem_limit_bytes=1 << 20),
            name="hold",
        )(value, *behind)

    def spread_mate(column, mate):
        return [mate, move(mate, "dp", ring(-1)), move(column[2], "dp", ring(0, 1)), move(mate, "dp", ring(-3))]

    def far_sum(keep, came, behind=()):
        low, high = call("far_sum", far_kernel, (keep, came), (shape(came.shape[0], columns // 2),) * 2, behind)
        return low, (up(low), down(high))

    def near_sum(keep, came, far, parts, behind=()):
        outs = [shape(rows, columns) for rows in parts for _ in range(2)]
        return call("near_sum", near_kernel, (keep, came, *far), tuple(outs), behind)

    def last_sum(near):
        return up(near[0]), down(near[1])

    def finish(at, low, keep, came, arrived, behind=()):
        rows = arrived[0].shape[0]
        return call(
            "residual",
            lambda *refs: finish_kernel(at, low, *refs),
            (keep, came, *arrived, residual_in),
            (shape(rows, columns), shape(rows, columns, jnp.float32)),
            behind,
            weigh=20,
        )

    local = call(
        "rotate_local",
        lambda *refs: rotate_kernel(scale, *refs),
        (attention_out, signs),
        tuple(shape(rows, width) for rows in ROWS),
        flops=2 * tokens * width * LANES,
    )
    other = [swap(local[0]), swap(local[1])]
    terms0 = near_z(pair(local[0], other[0]))
    ready = call("weight", touch_kernel, (out_weight,), shape(8, LANES), [terms0[0]], weigh=9)
    terms0 = far_z(terms0, [ready])
    terms1 = near_z(pair(local[1], other[1], [terms0[1]]))
    own0 = mix(terms0, [terms1[0]])
    column0, mate0 = spread_column(own0)
    mate0 = hold(mate0, [column0[1], column0[3]])
    mates0 = spread_mate(column0, mate0)
    own1 = mix(far_z(terms1), [mates0[1], mates0[3]])
    column1, mate1 = spread_column(own1)
    products0 = project(column0, out_weight, None, [own1])
    keep0, far0, near0 = project(mates0, out_weight, products0)
    mate1 = hold(mate1, [*column1[1:], keep0])
    far0 = swap(hold(far0, [mate1]))
    made0, ring0 = far_sum(keep0, far0)
    near0 = swap(hold(near0, [far0]))
    mates1 = spread_mate(column1, hold(mate1, [made0, near0]))
    sums0 = near_sum(keep0, near0, ring0, ROWS[:1])
    products1 = project(column1, out_weight, None, [sums0[0]])
    keep1, far1, near1 = project(mates1, out_weight, products1)
    last0 = last_sum(sums0)
    far1 = swap(hold(far1, last0))
    near1 = swap(hold(near1, [far1]))
    made1, ring1 = far_sum(keep1, far1)
    leading0, summed0 = finish(0, 0, keep0, near0, last0, [made1])
    passed0 = pipe(leading0)
    sums1 = near_sum(keep1, near1, ring1, PARTS)
    leading1, summed1 = finish(ROWS[0], 0, keep1, near1, last_sum(sums1[:2]), [leading0, passed0])
    passed1 = pipe(leading1)
    leading2, summed2 = finish(ROWS[0] + PARTS[0], PARTS[0], keep1, near1, last_sum(sums1[2:]), [leading1])
    passed2 = pipe(leading2)
    early = call(
        "early",
        early_kernel,
        (leading0, summed0, passed0, leading1, summed1, passed1),
        shape(tokens - PARTS[1], columns),
        weigh=20,
    )
    return call(
        "end",
        end_kernel,
        (early, leading2, summed2, passed2),
        jax.ShapeDtypeStruct((1, tokens, columns), BF16),
    )


def solution(mesh):
    in_specs = (
        P("pipe", "dp", "tensor"),
        P("pipe", "tensor"),
        P("pipe", "tensor", "dp"),
        P("tensor", "dp"),
    )
    out_specs = P("pipe", "tensor", "dp")
    return jax.shard_map(
        on_device, mesh=mesh, in_specs=in_specs, out_specs=out_specs, check_vma=False
    )
```
